32 devices in a mesh: head: 8 (over z, core), key: 4 (over y, x).
Axes of the slice: x: 2, y: 2, z: 4, core: 2. Of those that a mesh axis runs over, the one named last changes fastest.
Arguments:
- tokens: bfloat16 [4096, 2048], P(('head', 'key')), may hold values from -6 to 6
- upstream: bfloat16 [4096, 2048], P(('head', 'key')), may hold values from -6 to 6
- route_weight: float32 [4096, 8], P(('head', 'key')), may hold values from 0.02 to 0.5
- expert_ids: int32 [4096, 8], P(('head', 'key')), may hold values from 0 to 31, all different within a row; in each aligned block of 128 rows (0 to 127, 128 to 255, ...) at most 36 rows name the same one
- w_gate_up: bfloat16 [32, 2048, 1536], P(('head', 'key')), may hold values from -0.125 to 0.125
- w_down: bfloat16 [32, 768, 2048], P(('head', 'key')), may hold values from -0.21875 to 0.21875
- w_out: bfloat16 [4096, 2048], P('head'), may hold values from -0.09375 to 0.09375
- queries: bfloat16 [128, 4096], P(None, 'head'), may hold values from -4 to 4
- keys_values: bfloat16 [4096, 1024], P('key'), may hold values from -4 to 4
- key_blocks: int32 [32], P('key'), may hold values from 0 to 31, as said below
- attn_out: bfloat16 [128, 4096], P(None, 'head'), may hold values from -5 to 5, as said below
- attn_lse: float32 [32, 128], P('head'), may hold values from -200 to 200, as said below
Outputs:
- d_resid: bfloat16 [4096, 2048], P(('head', 'key'))
- grad_gate_up: bfloat16 [32, 2048, 1536], P(('head', 'key'))
- grad_down: bfloat16 [32, 768, 2048], P(('head', 'key'))
- grad_out: bfloat16 [4096, 2048], P('head', 'key')
- d_queries: bfloat16 [128, 4096], P('key', 'head')
- d_keys_values: bfloat16 [4096, 1024], P('key', 'head')
The draws below stay inside these ranges and needn't reach their ends.
Inputs may be any that keep to these rules, and one draw needn't show every extreme that they name: `expert_ids`: each row names 8 different experts; within one block of 128 rows no expert is named more than 36 times, and in some block one is named exactly 36 times. `key_blocks`: every block number appears once. `attn_out`: the forward attention output of these queries, keys and values under the causal rule of the steps, with probabilities rounded to bfloat16 before the product with values. `attn_lse`: the log of the sum over visible keys of exp of the scaled scores, for each head and query, as in the forward pass.
All inputs are finite; a program needn't handle non-finite values.
Results may differ from the reference program's by a relative error of at most 0.011.
Values may be sent and summed in bfloat16 or wider, within the bound.
No kernel may reach another device: no remote copies, remote signals or barrier semaphores. Data moves between devices by JAX's collectives and lax.ppermute only.
A program may use at most 192 MiB of HBM per device.

```python
import math
import jax
import jax.numpy as jnp
import numpy as np
from jax import lax

D = 2048
FF = 768
QH = 32
KVH = 4
HD = 128
TOPK = 8
TOK_DEV = 128
KBLK = 128
QLEN = 128
EXPERTS = 32
TOKENS = 4096
CAP = 36
KEYS = 4096
NB = 32
N_HEAD = 8
N_KEY = 4


def joint_draw(key):
    blocks = jax.random.permutation(jax.random.fold_in(key, 7001), NB).astype(jnp.int32)
    key_query = jax.random.fold_in(key, 7002)
    key_keys = jax.random.fold_in(key, 7003)
    key_values = jax.random.fold_in(key, 7004)
    query_part = jnp.clip(jax.random.normal(key_query, (QH, QLEN, HD), jnp.float32), -4.0, 4.0)
    key_part = jnp.clip(jax.random.normal(key_keys, (KVH, KEYS, HD), jnp.float32), -4.0, 4.0)
    value_part = jnp.clip(jax.random.normal(key_values, (KVH, KEYS, HD), jnp.float32), -4.0, 4.0)
    query_bf = query_part.astype(jnp.bfloat16)
    key_bf = key_part.astype(jnp.bfloat16)
    value_bf = value_part.astype(jnp.bfloat16)
    key_pos = (blocks[:, None] * KBLK + jnp.arange(KBLK, dtype=jnp.int32)[None, :]).reshape(KEYS)
    query_pos = KEYS - QLEN + jnp.arange(QLEN, dtype=jnp.int32)
    visible = key_pos[None, :] <= query_pos[:, None]
    group_size = QH // KVH

    def one_head(head_index):
        scores = jnp.dot(query_bf[head_index], key_bf[head_index // group_size].T, preferred_element_type=jnp.float32) * HD ** (-0.5)
        masked = jnp.where(visible, scores, -1e+30)
        row_top = jnp.max(masked, axis=1)
        weights = jnp.where(visible, jnp.exp(masked - row_top[:, None]), 0.0)
        row_total = jnp.sum(weights, axis=1)
        row_probs = (weights / row_total[:, None]).astype(jnp.bfloat16)
        output = jnp.dot(row_probs, value_bf[head_index // group_size], preferred_element_type=jnp.float32)
        return (output.astype(jnp.bfloat16), row_top + jnp.log(row_total))
    outputs, log_total = lax.map(one_head, jnp.arange(QH, dtype=jnp.int32))
    queries = query_bf.transpose(1, 0, 2).reshape(QLEN, QH * HD)
    keys_values = jnp.concatenate([key_bf.transpose(1, 0, 2).reshape(KEYS, KVH * HD), value_bf.transpose(1, 0, 2).reshape(KEYS, KVH * HD)], axis=1)
    attn_out = outputs.transpose(1, 0, 2).reshape(QLEN, QH * HD)
    return (queries, keys_values, blocks, attn_out, log_total)


def draw_queries(key, part):
    return joint_draw(key)[0]


def draw_keys_values(key, part):
    return joint_draw(key)[1]


def draw_key_blocks(key, part):
    return joint_draw(key)[2]


def draw_attn_out(key, part):
    return joint_draw(key)[3]


def draw_attn_lse(key, part):
    return joint_draw(key)[4]


def shard_levels(stream_key, extent, pieces, least, high):
    def one(axis_at, blocks):
        steps = jax.random.uniform(jax.random.fold_in(jax.random.fold_in(stream_key, 6), axis_at), (blocks,), jnp.float32, least / len(pieces), high / len(pieces))
        return jnp.repeat(jnp.exp(steps), extent[axis_at] // blocks).reshape((-1,) + (1,) * (len(extent) - axis_at - 1))

    loudness = one(*pieces[0])
    for cut in pieces[1:]:
        loudness = loudness * one(*cut)
    return loudness


def shared_out(own_key, own, number, rows, number_of, top, limit, skew):
    order = jax.random.permutation(own_key, number_of)
    heavy_load, usual = load_shares(number_of, rows * top, limit, skew, True), load_shares(number_of, rows * top, limit, skew, False)
    places = jnp.arange(number_of)

    def named(lengths, turn):
        used = int((lengths > 0).sum())
        fixed = max(1, used // 4)
        shifted = fixed + (places - fixed + turn * (used - fixed)) % max(1, number_of - fixed)
        return jnp.zeros((number_of,), jnp.int32).at[order[jnp.where(places < fixed, places, shifted)]].set(jnp.asarray(lengths, jnp.int32))

    lengths = jnp.where(number % 4 == 0, named(heavy_load, number // 4), named(usual, number - number // 4 - 1))
    mixed = jax.random.permutation(jax.random.fold_in(own, 3), number_of)
    donor, taker = mixed[0:number_of // 2 * 2:2], mixed[1:number_of // 2 * 2:2]
    room = jnp.minimum(lengths[donor] - 1, limit - lengths[taker]) // 2
    room = jnp.where((donor == order[0]) | (taker == order[0]) | (lengths[taker] == 0), 0, jnp.maximum(room, 0))
    shifted = jax.random.randint(jax.random.fold_in(own, 4), (number_of // 2,), 0, 1 << 20) % (room + 1)
    lengths = lengths.at[donor].add(-shifted).at[taker].add(shifted)
    members = jnp.searchsorted(jnp.cumsum(lengths), jnp.arange(rows * top), side="right").astype(jnp.int32)
    table = members.reshape(top, rows).T
    table = table[jax.random.permutation(jax.random.fold_in(own, 1), rows)]
    turn = jax.random.randint(jax.random.fold_in(own, 2), (rows, 1), 0, top)
    return jnp.take_along_axis(table, (jnp.arange(top)[None, :] + turn) % top, axis=1)


def load_shares(count, total, bound, skew, full):
    portions = [(1 << 20) // math.isqrt(standing ** skew) + 1 for standing in range(1, count + 1)]
    largest = bound if full else min(bound, max(-(-total // count), total * portions[0] // sum(portions)))
    least = 1 if total - largest >= count - 1 else 0
    counts, surplus = [largest] + [least] * (count - 1), total - largest - least * (count - 1)
    while surplus > 0:
        free = [i for i in range(1, count) if counts[i] < largest] or [i for i in range(1, count) if counts[i] < bound]
        whole, budget = sum([portions[i] for i in free]), surplus
        for i in free:
            extra = min(bound - counts[i], max(1, budget * portions[i] // whole), surplus)
            counts[i] = counts[i] + extra
            surplus = surplus - extra
    return np.array(counts)


def gaussian(own_key, dims, spread, most, split=(), held_as=jnp.bfloat16):
    level = shard_levels(own_key, dims, split, -0.22, 0.18) if split else 1.0
    array = jax.random.normal(own_key, dims, jnp.float32) * spread * level
    return jnp.minimum(jnp.maximum(array, -most), most).astype(held_as)


def setup_inputs(seed: int = 0) -> dict:
    splits = jax.random.split(jax.random.key(seed), 13)
    tokens = gaussian(splits[0], (TOKENS, D), 1.0, 6.0, ((0, 32),))
    upstream = gaussian(splits[1], (TOKENS, D), 1.0, 6.0, ((0, 32),))
    route_weight = jnp.clip(jnp.exp(math.log(0.5) - 3.218876 * jax.random.uniform(splits[2], (TOKENS, TOPK), jnp.float32) ** shard_levels(splits[2], (TOKENS, TOPK), ((0, 32),), -0.2, 0.2)), 0.02, 0.5)
    expert_ids_keys = jax.random.split(jax.random.fold_in(splits[3], 1), TOKENS // TOK_DEV)
    expert_ids_turns = jax.random.permutation(jax.random.fold_in(splits[3], 3), TOKENS // TOK_DEV)
    expert_ids = jax.vmap(lambda own, number: shared_out(jax.random.fold_in(splits[3], 2), own, number, TOK_DEV, EXPERTS, TOPK, CAP, 2))(expert_ids_keys, expert_ids_turns).reshape((TOKENS, TOPK))
    w_gate_up = gaussian(splits[4], (EXPERTS, D, 2 * FF), D ** -0.5, 0.125, ((0, 32),))
    w_down = gaussian(splits[5], (EXPERTS, FF, D), FF ** -0.5, 0.21875, ((0, 32),))
    w_out = gaussian(splits[6], (QH * HD, D), (QH * HD) ** -0.5, 0.09375, ((0, 8),))
    queries = draw_queries(jax.random.fold_in(splits[12], 71), 0)
    keys_values = draw_keys_values(jax.random.fold_in(splits[12], 71), 0)
    key_blocks = draw_key_blocks(jax.random.fold_in(splits[12], 71), 0)
    attn_out = draw_attn_out(jax.random.fold_in(splits[12], 71), 0)
    attn_lse = draw_attn_lse(jax.random.fold_in(splits[12], 71), 0)
    return {"tokens": tokens, "upstream": upstream, "route_weight": route_weight, "expert_ids": expert_ids, "w_gate_up": w_gate_up, "w_down": w_down, "w_out": w_out, "queries": queries, "keys_values": keys_values, "key_blocks": key_blocks, "attn_out": attn_out, "attn_lse": attn_lse}


def expert_backward(expert_in, scaled_in, weight_gate_up, weight_down):
    hidden_width = weight_down.shape[0]
    gate_up = jnp.dot(expert_in, weight_gate_up, preferred_element_type=jnp.float32)
    gate_part = gate_up[:, :hidden_width]
    up_part = gate_up[:, hidden_width:]
    gate_sigma = jax.nn.sigmoid(gate_part)
    activated = gate_part * gate_sigma
    hidden = (activated * up_part).astype(jnp.bfloat16)
    d_hidden = lax.dot_general(scaled_in, weight_down, (((1,), (1,)), ((), ())), preferred_element_type=jnp.float32)
    grad_down = lax.dot_general(hidden, scaled_in, (((0,), (0,)), ((), ())), preferred_element_type=jnp.float32).astype(jnp.bfloat16)
    d_gate = d_hidden * up_part * gate_sigma * (1.0 + gate_part * (1.0 - gate_sigma))
    d_up = d_hidden * activated
    d_gate_up = jnp.concatenate([d_gate, d_up], axis=1).astype(jnp.bfloat16)
    grad_gate_up = lax.dot_general(expert_in, d_gate_up, (((0,), (0,)), ((), ())), preferred_element_type=jnp.float32).astype(jnp.bfloat16)
    d_rows = lax.dot_general(d_gate_up, weight_gate_up, (((1,), (1,)), ((), ())), preferred_element_type=jnp.float32).astype(jnp.bfloat16)
    return grad_gate_up, grad_down, d_rows


def reference(tokens, upstream, route_weight, expert_ids, w_gate_up, w_down, w_out, queries, keys_values, key_blocks, attn_out, attn_lse):
    block_count = N_HEAD * N_KEY
    assigned = TOKENS * TOPK
    per_block = TOK_DEV * TOPK
    ids_block = expert_ids.reshape(block_count, per_block)
    onehot = (ids_block[:, :, None] == jnp.arange(EXPERTS, dtype=jnp.int32)[None, None, :]).astype(jnp.int32)
    position = (jnp.sum(jnp.cumsum(onehot, axis=1) * onehot, axis=2) - 1).astype(jnp.int32)
    slot = (jnp.arange(block_count, dtype=jnp.int32)[:, None] * CAP + position).reshape(assigned).astype(jnp.int32)
    flat_ids = expert_ids.reshape(assigned)
    slot_owner = jnp.full((EXPERTS, block_count * CAP), assigned, jnp.int32).at[flat_ids, slot].set(jnp.arange(assigned, dtype=jnp.int32))
    weight_pad = jnp.concatenate([route_weight.reshape(assigned), jnp.zeros((1,), jnp.float32)])
    zero_row = jnp.zeros((1, D), jnp.bfloat16)
    tokens_pad = jnp.concatenate([tokens, zero_row])
    upstream_pad = jnp.concatenate([upstream, zero_row])

    def expert_step(totals, expert):
        owners = slot_owner[expert]
        owner_rows = owners // TOPK
        expert_in = tokens_pad[owner_rows]
        scaled_in = (upstream_pad[owner_rows].astype(jnp.float32) * weight_pad[owners][:, None]).astype(jnp.bfloat16)
        grad_gate_up, grad_down, d_rows = expert_backward(expert_in, scaled_in, w_gate_up[expert], w_down[expert])
        totals = totals.at[owner_rows].add(d_rows.astype(jnp.float32))
        return totals, (grad_gate_up, grad_down)

    totals, (grad_gate_up, grad_down) = lax.scan(expert_step, jnp.zeros((TOKENS + 1, D), jnp.float32), jnp.arange(EXPERTS, dtype=jnp.int32))
    d_resid = (upstream.astype(jnp.float32) + totals[:TOKENS]).astype(jnp.bfloat16)

    window = d_resid[TOKENS - QLEN:]
    d_attn = jnp.dot(window, w_out.T, preferred_element_type=jnp.float32).astype(jnp.bfloat16)
    grad_out = jnp.dot(attn_out.T, window, preferred_element_type=jnp.float32).astype(jnp.bfloat16)

    key_pos = (key_blocks[:, None] * KBLK + jnp.arange(KBLK, dtype=jnp.int32)[None, :]).reshape(KEYS)
    query_pos = KEYS - QLEN + jnp.arange(QLEN, dtype=jnp.int32)
    visible = key_pos[None, :] <= query_pos[:, None]
    score_scale = HD ** -0.5
    group_size = QH // KVH
    query_heads = queries.reshape(QLEN, QH, HD).transpose(1, 0, 2)
    grad_heads = d_attn.reshape(QLEN, QH, HD).transpose(1, 0, 2)
    out_heads = attn_out.reshape(QLEN, QH, HD).transpose(1, 0, 2)
    key_heads = keys_values[:, :KVH * HD].reshape(KEYS, KVH, HD).transpose(1, 0, 2)
    value_heads = keys_values[:, KVH * HD:].reshape(KEYS, KVH, HD).transpose(1, 0, 2)

    def one_head(head_index):
        query_h = query_heads[head_index]
        grad_h = grad_heads[head_index]
        out_h = out_heads[head_index]
        key_h = key_heads[head_index // group_size]
        value_h = value_heads[head_index // group_size]
        scores = jnp.dot(query_h, key_h.T, preferred_element_type=jnp.float32) * score_scale
        soft_weights = jnp.where(visible, jnp.exp(scores - attn_lse[head_index][:, None]), 0.0)
        soft_bf = soft_weights.astype(jnp.bfloat16)
        row_delta = jnp.sum(grad_h.astype(jnp.float32) * out_h.astype(jnp.float32), axis=1)
        d_probs = jnp.dot(grad_h, value_h.T, preferred_element_type=jnp.float32)
        d_scores = (soft_weights * (d_probs - row_delta[:, None])).astype(jnp.bfloat16)
        d_query = jnp.dot(d_scores, key_h, preferred_element_type=jnp.float32) * score_scale
        d_key = jnp.dot(d_scores.T, query_h, preferred_element_type=jnp.float32) * score_scale
        d_value = jnp.dot(soft_bf.T, grad_h, preferred_element_type=jnp.float32)
        return d_query, d_key, d_value

    d_query_all, d_key_all, d_value_all = lax.map(one_head, jnp.arange(QH, dtype=jnp.int32))
    d_queries = d_query_all.transpose(1, 0, 2).reshape(QLEN, QH * HD).astype(jnp.bfloat16)
    key_sums = d_key_all.reshape(KVH, group_size, KEYS, HD).sum(axis=1).transpose(1, 0, 2).reshape(KEYS, KVH * HD)
    value_sums = d_value_all.reshape(KVH, group_size, KEYS, HD).sum(axis=1).transpose(1, 0, 2).reshape(KEYS, KVH * HD)
    d_keys_values = jnp.concatenate([key_sums, value_sums], axis=1).astype(jnp.bfloat16)
    return d_resid, grad_gate_up, grad_down, grad_out, d_queries, d_keys_values
```

```python
import jax
import jax.numpy as jnp
from jax import lax
from jax.sharding import PartitionSpec as P

QH = 32
KVH = 4
HD = 128
KBLK = 128

BF = jnp.bfloat16
F32 = jnp.float32


def dot(a, b, contract):
    return lax.dot_general(a, b, (contract, ((), ())), preferred_element_type=F32)


def swap(block, axis, mask):
    count = lax.axis_size(axis)
    return lax.ppermute(block, axis, [(i, i ^ mask) for i in range(count)])


def along_z(block, step):
    count = lax.axis_size("head")
    route = [(i, i + 2 * step) for i in range(count) if 0 <= i + 2 * step < count]
    return lax.ppermute(block, "head", route)


def pick(z, options):
    out = options[-1]
    for height in range(len(options) - 2, -1, -1):
        if options[height] is not out:
            out = jnp.where(z == height, options[height], out)
    return out


def gather_z(block, z, count):
    up, down = [block], [block]
    for _ in range(count - 1):
        up.append(along_z(up[-1], 1))
        down.append(along_z(down[-1], -1))
    blocks = [block]
    for mask in range(1, count):
        options = []
        for height in range(count):
            distance = (height ^ mask) - height
            options.append(down[distance] if distance > 0 else up[-distance])
        blocks.append(pick(z, options))
    return blocks


def last_to_all(block):
    n_head = lax.axis_size("head")
    n_key = lax.axis_size("key")
    axes = ("head", "key")
    me = lax.axis_index("head") * n_key + lax.axis_index("key")
    held = {n_head * n_key - 1}

    def send(block, move):
        route = [(i, move(i)) for i in sorted(held) if move(i) is not None]
        arrived = lax.ppermute(block, axes, route)
        takes = jnp.zeros((), jnp.bool_)
        for _, target in route:
            takes = takes | (me == target)
            held.add(target)
        return jnp.where(takes, arrived, block)

    bit = 1
    while bit < n_key:
        block = send(block, lambda i: i ^ bit)
        bit *= 2
    for height in range(n_head // 2 - 1, 0, -1):
        block = send(block, lambda i: i - 2 * n_key if i // (2 * n_key) == height else None)
    return send(block, lambda i: i ^ n_key)


def route_tables(ids, weights, first_expert, key, n_key):
    blocks, top, tokens = ids.shape
    experts = first_expert + jnp.bitwise_xor(key, jnp.arange(n_key, dtype=jnp.int32))
    hit = ids[:, None, :, :] == experts[None, :, None, None]
    chosen = jnp.any(hit, axis=2)
    weight = jnp.sum(jnp.where(hit, weights[:, None], 0.0), axis=2)
    order = jnp.arange(tokens, dtype=jnp.int32)
    before = (order[:, None] < order[None, :]).astype(BF)
    place = dot(chosen.reshape(blocks * n_key, tokens).astype(BF), before, ((1,), (0,)))
    place = place.reshape(blocks, n_key, tokens)
    return jnp.where(chosen, place, -1.0), weight


def shards(
    tokens,
    upstream,
    route_weight,
    expert_ids,
    w_gate_up,
    w_down,
    w_out,
    queries,
    keys_values,
    key_blocks,
    attn_out,
    attn_lse,
):
    tok_dev, d_model = tokens.shape
    top_count = expert_ids.shape[1]
    n_head = lax.axis_size("head")
    n_key = lax.axis_size("key")
    n_z = n_head // 2
    devices = n_head * n_key
    cap = max(2, 9 * tok_dev * top_count // (8 * devices))
    head = lax.axis_index("head")
    key = lax.axis_index("key")
    z = head // 2
    core = head % 2
    hidden_width = w_down.shape[1]
    gate_up_w = w_gate_up[0]
    down_w = w_down[0]

    info = jnp.concatenate([expert_ids.T.astype(F32), route_weight.T], axis=0)
    info_all = lax.all_gather(info, "head")
    place_all, weight_all = route_tables(
        info_all[:, :top_count].astype(jnp.int32),
        info_all[:, top_count:],
        head * n_key,
        key,
        n_key,
    )

    pair_slots = 2 * cap
    dest_rows = 2 * pair_slots
    sel_rows = n_key * dest_rows
    row = jnp.arange(sel_rows, dtype=jnp.int32)
    row_mask = row // dest_rows
    row_kind = row % dest_rows // pair_slots
    row_side = row % pair_slots // cap
    row_slot = row % cap
    col = jnp.arange(4 * tok_dev, dtype=jnp.int32)
    col_side = col // (2 * tok_dev)
    col_kind = col % (2 * tok_dev) // tok_dev
    row_pick = (row_mask[:, None] == jnp.arange(n_key)[None, :]).astype(BF)
    sel_meets = (row_kind[:, None] == col_kind[None, :]) & (row_side[:, None] == col_side[None, :])

    back_rows = n_key * pair_slots
    brow = jnp.arange(back_rows, dtype=jnp.int32)
    bcol = jnp.arange(2 * tok_dev, dtype=jnp.int32)
    back_pick = (brow[:, None] // pair_slots == jnp.arange(n_key)[None, :]).astype(BF)
    back_meets = (brow % pair_slots // cap)[:, None] == (bcol // tok_dev)[None, :]
    back_slot = brow % cap

    own = jnp.concatenate([tokens, upstream], axis=0)
    chunks = gather_z(own, z, n_z)

    kept = []
    returns = []
    for mask in range(n_z):
        source = jnp.bitwise_xor(z, mask) * 2
        mine, theirs = source + core, source + 1 - core
        place = jnp.stack([place_all[mine], place_all[theirs]], axis=1)
        weight = jnp.stack([weight_all[mine], weight_all[theirs]], axis=1)
        place_cols = jnp.broadcast_to(
            place[:, :, None, :], (n_key, 2, 2, tok_dev)
        ).reshape(n_key, 4 * tok_dev)
        weight_cols = jnp.broadcast_to(
            weight[:, :, None, :], (n_key, 2, 2, tok_dev)
        ).reshape(n_key, 4 * tok_dev)
        place_at = dot(row_pick, place_cols.astype(BF), ((1,), (0,)))
        chosen = (place_at == row_slot[:, None].astype(F32)) & sel_meets
        weight_at = lax.dot_general(
            row_pick.astype(F32),
            weight_cols,
            (((1,), (0,)), ((), ())),
            precision=lax.Precision.HIGHEST,
            preferred_element_type=F32,
        )
        scale = jnp.sum(jnp.where(chosen, weight_at, 0.0), axis=1)
        scale = jnp.where(row_kind == 0, 1.0, scale)
        chunk = chunks[mask]
        both = jnp.concatenate([chunk, swap(chunk, "head", 1)], axis=0)
        selected = dot(chosen.astype(BF), both, ((1,), (0,))) * scale[:, None]
        selected = selected.astype(BF)
        pieces = [selected[m * dest_rows : (m + 1) * dest_rows] for m in range(n_key)]
        pieces = [pieces[0]] + [swap(pieces[m], "key", m) for m in range(1, n_key)]
        expert_in = jnp.concatenate([p[:pair_slots] for p in pieces], axis=0)
        scaled_in = jnp.concatenate([p[pair_slots:] for p in pieces], axis=0)

        gate_up = dot(expert_in, gate_up_w, ((1,), (0,)))
        gate = gate_up[:, :hidden_width]
        up = gate_up[:, hidden_width:]
        sigma = jax.nn.sigmoid(gate)
        activated = gate * sigma
        hidden = (activated * up).astype(BF)
        d_hidden = dot(scaled_in, down_w, ((1,), (1,)))
        d_gate = d_hidden * up * sigma * (1.0 + gate * (1.0 - sigma))
        d_up = d_hidden * activated
        d_gate_up = jnp.concatenate([d_gate, d_up], axis=1).astype(BF)
        d_rows = dot(d_gate_up, gate_up_w, ((1,), (1,))).astype(BF)
        kept.append((expert_in, scaled_in, hidden, d_gate_up))

        back = [d_rows[m * pair_slots : (m + 1) * pair_slots] for m in range(n_key)]
        back = [back[0]] + [swap(back[m], "key", m) for m in range(1, n_key)]
        back = jnp.concatenate(back, axis=0)
        back_place = place.reshape(n_key, 2 * tok_dev).astype(BF)
        back_at = dot(back_pick, back_place, ((1,), (0,)))
        back_chosen = (back_at == back_slot[:, None].astype(F32)) & back_meets
        part = dot(back_chosen.astype(BF), back, ((0,), (0,)))
        total = part[:tok_dev] + swap(part[tok_dev:].astype(BF), "head", 1).astype(F32)
        returns.append(total)

    resid = upstream.astype(F32) + returns[0]
    for mask in range(1, n_z):
        resid = resid + swap(returns[mask].astype(BF), "head", 2 * mask).astype(F32)
    d_resid = resid.astype(BF)

    expert_in, scaled_in, hidden, d_gate_up = (
        jnp.concatenate([entry[i] for entry in kept], axis=0) for i in range(4)
    )
    grad_down = dot(hidden, scaled_in, ((0,), (0,))).astype(BF)
    grad_gate_up = dot(expert_in, d_gate_up, ((0,), (0,))).astype(BF)

    query_len = queries.shape[0]
    heads_dev = queries.shape[1] // HD
    key_dev = keys_values.shape[0]
    total_keys = key_dev * n_key
    score_scale = HD ** (-0.5)

    def by_head(x):
        return x.reshape(query_len, heads_dev, HD).transpose(1, 0, 2).reshape(-1, HD)

    kv_head = head * heads_dev // (QH // KVH)
    key_head = lax.dynamic_slice_in_dim(keys_values, kv_head * HD, HD, 1)
    value_head = lax.dynamic_slice_in_dim(keys_values, (KVH + kv_head) * HD, HD, 1)
    query_rows = by_head(queries)
    out_rows = by_head(attn_out)
    key_pos = (key_blocks[:, None] * KBLK + jnp.arange(KBLK, dtype=jnp.int32)[None, :]).reshape(
        key_dev
    )
    query_pos = total_keys - query_len + jnp.arange(query_len, dtype=jnp.int32)
    visible = key_pos[None, :] <= jnp.tile(query_pos, heads_dev)[:, None]
    scores = dot(query_rows, key_head, ((1,), (1,))) * score_scale
    probs = jnp.where(visible, jnp.exp(scores - attn_lse.reshape(-1)[:, None]), 0.0)

    window = last_to_all(d_resid)
    d_attn = dot(window, w_out, ((1,), (1,))).astype(BF)
    column_width = d_model // n_key
    columns = lax.dynamic_slice_in_dim(window, key * column_width, column_width, 1)
    grad_out = dot(attn_out, columns, ((0,), (0,))).astype(BF)
    grad_rows = by_head(d_attn)
    delta = jnp.sum(grad_rows.astype(F32) * out_rows.astype(F32), axis=1)
    d_probs = dot(grad_rows, value_head, ((1,), (1,)))
    d_scores = (probs * (d_probs - delta[:, None])).astype(BF)
    d_query = dot(d_scores, key_head, ((1,), (0,))) * score_scale
    d_key = dot(d_scores, query_rows, ((0,), (0,))) * score_scale
    d_value = dot(probs.astype(BF), grad_rows, ((0,), (0,)))

    first = core == 0
    held = jnp.where(first, d_key, d_value)
    other = jnp.where(first, d_value, d_key).astype(BF)
    held = (held + swap(other, "head", 1).astype(F32)).astype(BF)
    to_owner = [(i, i % 2 * KVH + i // 2) for i in range(n_head)]
    d_keys_values = lax.ppermute(held, "head", to_owner)

    d_query = d_query.reshape(heads_dev, query_len, HD).transpose(1, 0, 2)
    d_query = d_query.reshape(query_len, heads_dev * HD)
    share = query_len // n_key
    d_queries = lax.dynamic_slice_in_dim(d_query, key * share, share, 0)
    for m in range(1, n_key):
        part = lax.dynamic_slice_in_dim(d_query, jnp.bitwise_xor(key, m) * share, share, 0)
        d_queries = d_queries + swap(part, "key", m)
    return (
        d_resid,
        grad_gate_up[None],
        grad_down[None],
        grad_out,
        d_queries.astype(BF),
        d_keys_values,
    )


def solution(mesh):
    return jax.shard_map(
        shards,
        mesh=mesh,
        in_specs=(
            P(("head", "key"), None),
            P(("head", "key"), None),
            P(("head", "key"), None),
            P(("head", "key"), None),
            P(("head", "key"), None, None),
            P(("head", "key"), None, None),
            P("head", None),
            P(None, "head"),
            P("key", None),
            P("key"),
            P(None, "head"),
            P("head", None),
        ),
        out_specs=(
            P(("head", "key"), None),
            P(("head", "key"), None, None),
            P(("head", "key"), None, None),
            P("head", "key"),
            P("key", "head"),
            P("key", "head"),
        ),
        check_vma=False,
    )
```

```python
import functools

import jax
import jax.numpy as jnp
from jax import lax
from jax.experimental import pallas as pl
from jax.experimental.pallas import tpu as pltpu
from jax.sharding import PartitionSpec as P

QH = 32
KVH = 4
HD = 128
KBLK = 128

BF = jnp.bfloat16
F32 = jnp.float32


def dot(a, b, contract):
    return lax.dot_general(a, b, (contract, ((), ())), preferred_element_type=F32)


HEAD = ("z", "core")


def swap(block, axis, mask):
    count = lax.axis_size(axis)
    return lax.ppermute(block, axis, [(i, i ^ mask) for i in range(count)])


def along_z(block, step):
    count = lax.axis_size(HEAD)
    route = [(i, i + 2 * step) for i in range(count) if 0 <= i + 2 * step < count]
    return lax.ppermute(block, HEAD, route)


def pick(z, options):
    out = options[-1]
    for height in range(len(options) - 2, -1, -1):
        if options[height] is not out:
            out = jnp.where(z == height, options[height], out)
    return out


def gather_z(block, z, count):
    up, down = [block], [block]
    for _ in range(count - 1):
        up.append(along_z(up[-1], 1))
        down.append(along_z(down[-1], -1))
    blocks = [block]
    for mask in range(1, count):
        options = []
        for height in range(count):
            distance = (height ^ mask) - height
            options.append(down[distance] if distance > 0 else up[-distance])
        blocks.append(pick(z, options))
    return blocks


def last_to_all(block):
    n_head = lax.axis_size(HEAD)
    n_key = lax.axis_size("key")
    axes = ("z", "core", "key")
    me = lax.axis_index(HEAD) * n_key + lax.axis_index("key")
    held = {n_head * n_key - 1}

    def send(block, move):
        route = [(i, move(i)) for i in sorted(held) if move(i) is not None]
        arrived = lax.ppermute(block, axes, route)
        takes = jnp.zeros((), jnp.bool_)
        for _, target in route:
            takes = takes | (me == target)
            held.add(target)
        return jnp.where(takes, arrived, block)

    bit = 1
    while bit < n_key:
        block = send(block, lambda i: i ^ bit)
        bit *= 2
    for height in range(n_head // 2 - 1, 0, -1):
        block = send(block, lambda i: i - 2 * n_key if i // (2 * n_key) == height else None)
    return send(block, lambda i: i ^ n_key)


def route_tables(ids, weights, first_expert, key, n_key):
    blocks, top, tokens = ids.shape
    experts = first_expert + jnp.bitwise_xor(key, jnp.arange(n_key, dtype=jnp.int32))
    hit = ids[:, None, :, :] == experts[None, :, None, None]
    chosen = jnp.any(hit, axis=2)
    weight = jnp.sum(jnp.where(hit, weights[:, None], 0.0), axis=2)
    order = jnp.arange(tokens, dtype=jnp.int32)
    before = (order[:, None] < order[None, :]).astype(BF)
    place = dot(chosen.reshape(blocks * n_key, tokens).astype(BF), before, ((1,), (0,)))
    place = place.reshape(blocks, n_key, tokens)
    return jnp.where(chosen, place, -1.0), weight


def layer_plain(tokens, upstream, route_weight, expert_ids, w_gate_up, w_down, early, attend):
    tok_dev, d_model = tokens.shape
    top_count = expert_ids.shape[1]
    n_head = lax.axis_size(HEAD)
    n_key = lax.axis_size("key")
    n_z = n_head // 2
    devices = n_head * n_key
    cap = max(2, 9 * tok_dev * top_count // (8 * devices))
    head = lax.axis_index(HEAD)
    key = lax.axis_index("key")
    z = head // 2
    core = head % 2
    hidden_width = w_down.shape[0]

    info = jnp.concatenate([expert_ids.T.astype(F32), route_weight.T], axis=0)
    info_all = lax.all_gather(info, HEAD)
    place_all, weight_all = route_tables(
        info_all[:, :top_count].astype(jnp.int32),
        info_all[:, top_count:],
        head * n_key,
        key,
        n_key,
    )

    pair_slots = 2 * cap
    dest_rows = 2 * pair_slots
    sel_rows = n_key * dest_rows
    row = jnp.arange(sel_rows, dtype=jnp.int32)
    row_mask = row // dest_rows
    row_kind = row % dest_rows // pair_slots
    row_side = row % pair_slots // cap
    row_slot = row % cap
    col = jnp.arange(4 * tok_dev, dtype=jnp.int32)
    col_side = col // (2 * tok_dev)
    col_kind = col % (2 * tok_dev) // tok_dev
    row_pick = (row_mask[:, None] == jnp.arange(n_key)[None, :]).astype(BF)
    sel_meets = (row_kind[:, None] == col_kind[None, :]) & (row_side[:, None] == col_side[None, :])

    back_rows = n_key * pair_slots
    brow = jnp.arange(back_rows, dtype=jnp.int32)
    bcol = jnp.arange(2 * tok_dev, dtype=jnp.int32)
    back_pick = (brow[:, None] // pair_slots == jnp.arange(n_key)[None, :]).astype(BF)
    back_meets = (brow % pair_slots // cap)[:, None] == (bcol // tok_dev)[None, :]
    back_slot = brow % cap

    own = jnp.concatenate([tokens, upstream], axis=0)
    chunks = gather_z(own, z, n_z)

    kept = []
    returns = []
    for mask in range(n_z):
        source = jnp.bitwise_xor(z, mask) * 2
        mine, theirs = source + core, source + 1 - core
        place = jnp.stack([place_all[mine], place_all[theirs]], axis=1)
        weight = jnp.stack([weight_all[mine], weight_all[theirs]], axis=1)
        place_cols = jnp.broadcast_to(
            place[:, :, None, :], (n_key, 2, 2, tok_dev)
        ).reshape(n_key, 4 * tok_dev)
        weight_cols = jnp.broadcast_to(
            weight[:, :, None, :], (n_key, 2, 2, tok_dev)
        ).reshape(n_key, 4 * tok_dev)
        place_at = dot(row_pick, place_cols.astype(BF), ((1,), (0,)))
        chosen = (place_at == row_slot[:, None].astype(F32)) & sel_meets
        weight_at = lax.dot_general(
            row_pick.astype(F32),
            weight_cols,
            (((1,), (0,)), ((), ())),
            precision=lax.Precision.HIGHEST,
            preferred_element_type=F32,
        )
        scale = jnp.sum(jnp.where(chosen, weight_at, 0.0), axis=1)
        scale = jnp.where(row_kind == 0, 1.0, scale)
        chunk = chunks[mask]
        both = jnp.concatenate([chunk, swap(chunk, "core", 1)], axis=0)
        selected = dot(chosen.astype(BF), both, ((1,), (0,))) * scale[:, None]
        selected = selected.astype(BF)
        pieces = [selected[m * dest_rows : (m + 1) * dest_rows] for m in range(n_key)]
        pieces = [pieces[0]] + [swap(pieces[m], "key", m) for m in range(1, n_key)]
        expert_in = jnp.concatenate([p[:pair_slots] for p in pieces], axis=0)
        scaled_in = jnp.concatenate([p[pair_slots:] for p in pieces], axis=0)

        gate_up = dot(expert_in, w_gate_up, ((1,), (0,)))
        gate = gate_up[:, :hidden_width]
        up = gate_up[:, hidden_width:]
        sigma = jax.nn.sigmoid(gate)
        activated = gate * sigma
        hidden = (activated * up).astype(BF)
        d_hidden = dot(scaled_in, w_down, ((1,), (1,)))
        d_gate = d_hidden * up * sigma * (1.0 + gate * (1.0 - sigma))
        d_up = d_hidden * activated
        d_gate_up = jnp.concatenate([d_gate, d_up], axis=1).astype(BF)
        d_rows = dot(d_gate_up, w_gate_up, ((1,), (1,))).astype(BF)
        kept.append((expert_in, scaled_in, hidden, d_gate_up))

        back = [d_rows[m * pair_slots : (m + 1) * pair_slots] for m in range(n_key)]
        back = [back[0]] + [swap(back[m], "key", m) for m in range(1, n_key)]
        back = jnp.concatenate(back, axis=0)
        back_place = place.reshape(n_key, 2 * tok_dev).astype(BF)
        back_at = dot(back_pick, back_place, ((1,), (0,)))
        back_chosen = (back_at == back_slot[:, None].astype(F32)) & back_meets
        part = dot(back_chosen.astype(BF), back, ((0,), (0,)))
        total = part[:tok_dev] + swap(part[tok_dev:].astype(BF), "core", 1).astype(F32)
        returns.append(total)

    resid = upstream.astype(F32) + returns[0]
    for mask in range(1, n_z):
        resid = resid + swap(returns[mask].astype(BF), "z", mask).astype(F32)
    d_resid = resid.astype(BF)

    expert_in, scaled_in, hidden, d_gate_up = (
        jnp.concatenate([entry[i] for entry in kept], axis=0) for i in range(4)
    )
    grad_down = dot(hidden, scaled_in, ((0,), (0,))).astype(BF)
    grad_gate_up = dot(expert_in, d_gate_up, ((0,), (0,))).astype(BF)
    return (d_resid, grad_gate_up, grad_down, *attend(last_to_all(d_resid))[0])


INFO_ROWS = 16
VMEM_LIMIT = 56 * 2**20


def params():
    return pltpu.CompilerParams(vmem_limit_bytes=VMEM_LIMIT)


def cost():
    return pl.CostEstimate(flops=1000, bytes_accessed=1000, transcendentals=0)


ANY = pl.BlockSpec(memory_space=pl.ANY)


def build_kernel(ids_ref, weight_ref, tokens_ref, out_ref):
    rows = tokens_ref.shape[0]
    out_ref[:rows] = tokens_ref[...]
    weight = weight_ref[...]
    high = weight.astype(BF).astype(F32)
    middle = (weight - high).astype(BF).astype(F32)
    low = weight - high - middle
    parts = jnp.concatenate([ids_ref[...].astype(F32), high, middle, low], axis=1)
    parts = jnp.concatenate([parts, jnp.zeros_like(parts)], axis=0)
    out_ref[rows:] = jnp.zeros((INFO_ROWS, out_ref.shape[1]), BF)
    out_ref[rows:, : parts.shape[1]] = parts.astype(BF)


def build(ids, weights, tokens):
    rows, width = tokens.shape
    return pl.pallas_call(
        build_kernel,
        out_shape=jax.ShapeDtypeStruct((rows + INFO_ROWS, width), BF),
        compiler_params=params(),
        cost_estimate=cost(),
        name="build_block",
    )(ids, weights, tokens)


def select_kernel(n_key, cap, top, rows, meta, xa, xb, ia, ib, after, out_ref, hot_out, scale_out, hot_ref):
    slots = 2 * cap

    @pl.when(pl.program_id(1) == 0)
    def _():
        order = lax.broadcasted_iota(jnp.int32, (rows, rows), 0)
        later = lax.broadcasted_iota(jnp.int32, (rows, rows), 1)
        before = jnp.where(order < later, 1.0, 0.0).astype(BF)
        places, scales = [], []
        for ref in (ia, ib):
            info = ref[...].astype(F32)[:top]
            ids = info[:, :rows]
            weight = info[:, rows : 2 * rows] + info[:, 2 * rows : 3 * rows]
            weight = weight + info[:, 3 * rows : 4 * rows]
            chosen, scale = [], []
            for m in range(n_key):
                expert = (meta[0] + m).astype(F32)
                hit = ids == expert
                chosen.append(jnp.max(jnp.where(hit, 1.0, 0.0), axis=0, keepdims=True))
                scale.append(jnp.sum(jnp.where(hit, weight, 0.0), axis=0, keepdims=True))
            chosen = jnp.concatenate(chosen, axis=0)
            place = jnp.dot(chosen.astype(BF), before, preferred_element_type=F32)
            places.append(jnp.where(chosen > 0.0, place, -1.0e6))
            scales.append(scale)
        row = lax.broadcasted_iota(jnp.int32, (n_key * slots, 2 * rows), 0).astype(F32)
        hot = jnp.zeros((n_key * slots, 2 * rows), F32)
        weighted = jnp.zeros((n_key * slots, 2 * rows), F32)
        for m in range(n_key):
            at = jnp.concatenate([places[0][m : m + 1], places[1][m : m + 1] + cap], axis=1)
            scale = jnp.concatenate([scales[0][m], scales[1][m]], axis=1)
            hit = row == at + m * slots
            hot = jnp.where(hit, 1.0, hot)
            weighted = jnp.where(hit, scale, weighted)
        hot_ref[...] = hot.astype(BF)
        hot_out[...] = hot.astype(BF)
        total = jnp.sum(weighted, axis=1, keepdims=True)
        scale_out[...] = jnp.broadcast_to(total, scale_out.shape)

    values = jnp.concatenate([xa[:rows], xb[:rows]], axis=0)
    inputs = jnp.dot(hot_ref[...], values, preferred_element_type=F32)
    for m in range(n_key):
        out_ref[m] = inputs[m * slots : (m + 1) * slots].astype(BF)


def select(meta, count, mine, theirs, n_key, cap, top, tile, after):
    _, total, width = mine.shape
    rows = total - INFO_ROWS
    slots = 2 * cap
    tile = min(tile, width)
    at_info = rows // INFO_ROWS
    return pl.pallas_call(
        functools.partial(select_kernel, n_key, cap, top, rows),
        grid_spec=pltpu.PrefetchScalarGridSpec(
            num_scalar_prefetch=1,
            grid=(count, width // tile),
            in_specs=[
                pl.BlockSpec((None, total, tile), lambda j, i, meta: (meta[j + 1], 0, i)),
                pl.BlockSpec((None, total, tile), lambda j, i, meta: (meta[j + 1], 0, i)),
                pl.BlockSpec(
                    (None, INFO_ROWS, 4 * rows), lambda j, i, meta: (meta[j + 1], at_info, 0)
                ),
                pl.BlockSpec(
                    (None, INFO_ROWS, 4 * rows), lambda j, i, meta: (meta[j + 1], at_info, 0)
                ),
                ANY,
            ],
            out_specs=[
                pl.BlockSpec((n_key, None, slots, tile), lambda j, i, meta: (0, j, 0, i)),
                pl.BlockSpec((None, n_key * slots, 2 * rows), lambda j, i, meta: (j, 0, 0)),
                pl.BlockSpec((None, n_key * slots, 128), lambda j, i, meta: (j, 0, 0)),
            ],
            scratch_shapes=[pltpu.VMEM((n_key * slots, 2 * rows), BF)],
        ),
        out_shape=[
            jax.ShapeDtypeStruct((n_key, count, slots, width), BF),
            jax.ShapeDtypeStruct((count, n_key * slots, 2 * rows), BF),
            jax.ShapeDtypeStruct((count, n_key * slots, 128), F32),
        ],
        compiler_params=params(),
        cost_estimate=cost(),
        name="select_inputs",
    )(meta, mine, theirs, mine, theirs, after)


def scaled_kernel(n_key, meta, xa, xb, hot_ref, scale_ref, after, out_ref):
    slots = out_ref.shape[1]
    values = jnp.concatenate([xa[...], xb[...]], axis=0)
    rows = jnp.dot(hot_ref[...], values, preferred_element_type=F32) * scale_ref[:, :1]
    for m in range(n_key):
        out_ref[m] = rows[m * slots : (m + 1) * slots].astype(BF)


def select_scaled(meta, chunk, mine, theirs, hots, scales, n_key, tile, after):
    _, rows, width = mine.shape
    slots = hots.shape[1] // n_key
    tile = min(tile, width)
    block = pl.BlockSpec((None, rows, tile), lambda i, meta: (meta[chunk + 1], 0, i))
    return pl.pallas_call(
        functools.partial(scaled_kernel, n_key),
        grid_spec=pltpu.PrefetchScalarGridSpec(
            num_scalar_prefetch=1,
            grid=(width // tile,),
            in_specs=[
                block,
                block,
                pl.BlockSpec((None, n_key * slots, 2 * rows), lambda i, meta: (chunk, 0, 0)),
                pl.BlockSpec((None, n_key * slots, 128), lambda i, meta: (chunk, 0, 0)),
                ANY,
            ],
            out_specs=pl.BlockSpec((n_key, slots, tile), lambda i, meta: (0, 0, i)),
        ),
        out_shape=jax.ShapeDtypeStruct((n_key, slots, width), BF),
        compiler_params=params(),
        cost_estimate=cost(),
        name="select_scaled",
    )(meta, mine, theirs, hots, scales, after)


def gate_kernel(n_key, count, pieces, gate_w, up_w, *refs):
    in_ref, gate_ref, up_ref = refs[-3:]

    @pl.when(pl.program_id(0) == 0)
    def _():
        for j in range(count):
            joined = jnp.concatenate([pieces[m, j].astype(F32) for m in range(n_key)], axis=0)
            rows = joined.shape[0]
            in_ref[j * rows : (j + 1) * rows] = joined.astype(BF)

    gate_ref[...] = jnp.dot(in_ref[...], gate_w[...], preferred_element_type=F32)
    up_ref[...] = jnp.dot(in_ref[...], up_w[...], preferred_element_type=F32)


def gate_up(pieces, w_gate_up, hidden, tile, total, at, into, after):
    n_key, count, slots, width = pieces.shape
    rows = count * n_key * slots
    steps = hidden // tile
    part = pl.BlockSpec((rows, tile), lambda i: (0, i))
    return pl.pallas_call(
        functools.partial(gate_kernel, n_key, count),
        grid=(steps,),
        out_shape=[
            jax.ShapeDtypeStruct((total, width), BF),
            jax.ShapeDtypeStruct((rows, hidden), F32),
            jax.ShapeDtypeStruct((rows, hidden), F32),
        ],
        in_specs=[
            pl.BlockSpec((n_key, count, slots, width), lambda i: (0, 0, 0, 0)),
            pl.BlockSpec((width, tile), lambda i: (0, i)),
            pl.BlockSpec((width, tile), lambda i: (0, steps + i)),
            ANY,
        ]
        + [ANY] * len(into),
        out_specs=[pl.BlockSpec((rows, width), lambda i: (at, 0)), part, part],
        input_output_aliases={4 + i: i for i in range(len(into))},
        compiler_params=params(),
        cost_estimate=cost(),
        name="gate_up",
    )(pieces, w_gate_up, w_gate_up, after, *into)


def expert_kernel(n_key, meta, pieces, gate_in, up_in, gate_w, up_w, down_w, *refs):
    outs = refs[-n_key - 5 : -5]
    scaled_ref, hidden_ref, d_gate_ref, d_up_ref, total_ref = refs[-5:]
    slots = pieces.shape[1]
    step = pl.program_id(0)

    @pl.when(step == 0)
    def _():
        joined = jnp.concatenate([pieces[m].astype(F32) for m in range(n_key)], axis=0)
        scaled_ref[...] = joined.astype(BF)

    nt = (((1,), (1,)), ((), ()))
    gate, up = gate_in[...], up_in[...]
    d_hidden = lax.dot_general(scaled_ref[...], down_w[...], nt, preferred_element_type=F32)
    sigma = jax.nn.sigmoid(gate)
    activated = gate * sigma
    hidden_ref[...] = (activated * up).astype(BF)
    d_gate = (d_hidden * up * sigma * (1.0 + gate * (1.0 - sigma))).astype(BF)
    d_up = (d_hidden * activated).astype(BF)
    d_gate_ref[...] = d_gate
    d_up_ref[...] = d_up
    part = lax.dot_general(d_gate, gate_w[...], nt, preferred_element_type=F32)
    part = part + lax.dot_general(d_up, up_w[...], nt, preferred_element_type=F32)

    @pl.when(step == 0)
    def _():
        total_ref[...] = part

    @pl.when(step > 0)
    def _():
        total_ref[...] += part

    @pl.when(step == pl.num_programs(0) - 1)
    def _():
        for m in range(n_key):
            start = pl.multiple_of(jnp.bitwise_xor(meta[0], m) * slots, 8)
            outs[m][...] = total_ref[pl.ds(start, slots)].astype(BF)


def expert(meta, pieces, gate, up, chunk, w_gate_up, w_down, tile, at, chunks, kept, after):
    n_key, slots, width = pieces.shape
    hidden = w_down.shape[0]
    rows = n_key * slots
    steps = hidden // tile
    piece = pl.BlockSpec((n_key, slots, width), lambda i: (0, 0, 0))
    came = pl.BlockSpec((rows, tile), lambda i: (chunk, i))
    part = pl.BlockSpec((rows, tile), lambda i: (at, i))
    outs = pl.pallas_call(
        functools.partial(expert_kernel, n_key),
        grid=(steps,),
        out_shape=[jax.ShapeDtypeStruct((slots, width), BF)] * n_key
        + [jax.ShapeDtypeStruct((chunks * rows, width), BF)]
        + [jax.ShapeDtypeStruct((chunks * rows, hidden), BF)] * 3,
        in_specs=[
            pl.BlockSpec(memory_space=pltpu.SMEM),
            piece,
            came,
            came,
            pl.BlockSpec((width, tile), lambda i: (0, i)),
            pl.BlockSpec((width, tile), lambda i: (0, steps + i)),
            pl.BlockSpec((tile, width), lambda i: (i, 0)),
        ]
        + [ANY] * (len(kept) + 1),
        out_specs=[pl.BlockSpec((slots, width), lambda i: (0, 0))] * n_key
        + [pl.BlockSpec((rows, width), lambda i: (at, 0))]
        + [part] * 3,
        input_output_aliases={7 + i: n_key + i for i in range(len(kept))},
        scratch_shapes=[pltpu.VMEM((rows, width), F32)],
        compiler_params=params(),
        cost_estimate=cost(),
        name="expert_chunk",
    )(meta, pieces, gate, up, w_gate_up, w_gate_up, w_down, *kept, after)
    return list(outs[:n_key]), list(outs[n_key:])


def weights_kernel(left_ref, right_ref, *refs):
    out_ref, done_ref = refs[-2:]
    out_ref[...] = lax.dot_general(
        left_ref[...], right_ref[...], (((0,), (0,)), ((), ())), preferred_element_type=F32
    ).astype(BF)
    done_ref[...] = jnp.zeros_like(done_ref)


def weight_grad(left, right, tile, after, part=0, parts=1, into=None):
    rows, height = left.shape
    width = right.shape[1]
    aliased = [] if into is None else [into]
    return pl.pallas_call(
        weights_kernel,
        grid=(height // tile,),
        out_shape=[
            jax.ShapeDtypeStruct((height, parts * width), BF),
            jax.ShapeDtypeStruct((8, 128), F32),
        ],
        in_specs=[
            pl.BlockSpec((rows, tile), lambda i: (0, i)),
            pl.BlockSpec((rows, width), lambda i: (0, 0)),
            ANY,
        ]
        + [ANY] * len(aliased),
        out_specs=[
            pl.BlockSpec((tile, width), lambda i: (i, part)),
            pl.BlockSpec((8, 128), lambda i: (0, 0)),
        ],
        input_output_aliases={3: 0} if aliased else {},
        compiler_params=params(),
        cost_estimate=cost(),
        name="weight_gradient",
    )(left, right, after, *aliased)


def combine_kernel(n_key, meta, hot_ref, *refs):
    backs = refs[:n_key]
    keep_ref, send_ref, joined_ref = refs[n_key + 1 :]
    rows = keep_ref.shape[0]
    slots = backs[0].shape[0]
    tn = (((0,), (0,)), ((), ()))
    for m in range(n_key):
        start = pl.multiple_of(jnp.bitwise_xor(meta[0], m) * slots, 8)
        joined_ref[pl.ds(start, slots)] = backs[m][...].astype(F32)
    total = lax.dot_general(
        hot_ref[...], joined_ref[...].astype(BF), tn, preferred_element_type=F32
    )
    keep_ref[...] = total[:rows]
    send_ref[...] = total[rows:].astype(BF)


def combine(meta, hots, chunk, backs, tile, after):
    n_key = len(backs)
    slots, width = backs[0].shape
    tokens = hots.shape[2]
    rows = tokens // 2
    tile = min(tile, width)
    return pl.pallas_call(
        functools.partial(combine_kernel, n_key),
        grid=(width // tile,),
        out_shape=[
            jax.ShapeDtypeStruct((rows, width), F32),
            jax.ShapeDtypeStruct((rows, width), BF),
        ],
        in_specs=[
            pl.BlockSpec(memory_space=pltpu.SMEM),
            pl.BlockSpec((None, n_key * slots, tokens), lambda i: (chunk, 0, 0)),
        ]
        + [pl.BlockSpec((slots, tile), lambda i: (0, i))] * n_key
        + [ANY],
        out_specs=[pl.BlockSpec((rows, tile), lambda i: (0, i))] * 2,
        scratch_shapes=[pltpu.VMEM((n_key * slots, tile), F32)],
        compiler_params=params(),
        cost_estimate=cost(),
        name="combine_rows",
    )(meta, hots, *backs, after)


ORDER = ((3, 1, 2), (3, 2, 0), (3, 0, 1), (0, 1, 2))


def layer(tokens, upstream, route_weight, expert_ids, w_gate_up, w_down, early, attend):
    n_key = lax.axis_size("key")
    n_z = lax.axis_size("z")
    tok_dev = tokens.shape[0]
    top_count = expert_ids.shape[1]
    cap = max(2, 9 * tok_dev * top_count // (16 * n_z * n_key))
    head = lax.axis_index(HEAD)
    core = lax.axis_index("core")
    z = lax.axis_index("z")
    key = lax.axis_index("key")
    key_meta = key.astype(jnp.int32)[None]
    rows = n_key * 2 * cap
    hidden_width = w_down.shape[0]
    block = build(expert_ids.T, route_weight.T, tokens)
    column = lax.all_gather(block, "z")
    column_up = lax.all_gather(upstream, "z")
    state = {"after": block}
    hots, backs, parts, kept, totals = {}, {}, {}, [], {}

    def after(x, *others):
        return lax.optimization_barrier((x, *others))[0]

    def exchange(x):
        return lax.all_to_all(x, "key", split_axis=0, concat_axis=0, tiled=True)

    def run_inputs(heights, mine, theirs):
        meta = jnp.stack([head * n_key] + heights).astype(jnp.int32)
        out = select(
            meta, len(heights), mine, theirs, n_key, cap, top_count, 1024, state["after"]
        )
        state["after"] = out[1]
        return (meta, *out)

    def run_scaled(meta, chunk, mine, theirs, hots, scales):
        out = select_scaled(
            meta,
            chunk,
            mine,
            theirs,
            hots,
            scales,
            n_key,
            1024,
            state["after"],
        )
        state["after"] = out
        return exchange(out)

    def run_gate(pieces, at, into, tile):
        out = gate_up(
            pieces, w_gate_up, hidden_width, tile, n_z * rows, at, into, state["after"]
        )
        state["after"] = out[1]
        return out

    def run_expert(m, pieces, gate, up):
        out, kept[:] = expert(
            key_meta,
            pieces,
            gate,
            up,
            max(m - 1, 0),
            w_gate_up,
            w_down,
            hidden_width,
            (m - 1) % n_z,
            n_z,
            list(kept),
            state["after"],
        )
        state["after"] = out[0]
        backs[m] = [out[0]] + [swap(out[i], "key", i) for i in range(1, n_key)]

    def run_combine(m):
        parts[m] = combine(
            key_meta, hots[min(m, 1)], max(m - 1, 0), backs[m], 1024, state["after"]
        )
        state["after"] = parts[m][0]

    def run_total(m):
        keep, send = parts[m]
        totals[m] = keep + swap(send, "core", 1).astype(F32)
        totals[m] = totals[m] if m == 0 else totals[m].astype(BF)

    def pass_z(block, route):
        return lax.ppermute(block, "z", route)

    def then(*others):
        state["after"] = after(state["after"], *others)

    near, near2 = block[None], swap(block, "core", 1)[None]
    meta, inputs, hots[0], scales = run_inputs([z * 0], near, near2)
    inputs = exchange(inputs)
    near, near2 = upstream[None], swap(upstream, "core", 1)[None]
    scaled = run_scaled(meta, 0, near, near2, hots[0], scales)
    ins, gate, up = run_gate(inputs, n_z - 1, [], 384)
    run_expert(0, scaled, gate, up)
    column = after(column, state["after"], *early)
    heights = [pick(z, [jnp.int32(order[j]) for order in ORDER]) for j in range(n_z - 1)]
    meta, inputs, hots[1], scales = run_inputs(heights, column, swap(column, "core", 1))
    inputs = exchange(after(inputs, *backs[0]))
    column_up = after(column_up, state["after"])
    column_up2 = swap(column_up, "core", 1)
    scaled = {}

    def fetch_scaled(m):
        scaled[m] = run_scaled(meta, m - 1, column_up, column_up2, hots[1], scales)

    fetch_scaled(1)
    ins, gate, up = run_gate(inputs, 0, [ins], 256)
    fetch_scaled(2)
    run_expert(1, scaled[1], gate, up)
    fetch_scaled(3)
    run_combine(0)
    run_expert(2, scaled[2], gate, up)
    then(scaled[3])
    run_combine(1)

    last = z == n_z - 1
    partial = jnp.where(head * n_key + key == 2 * n_z * n_key - 1, upstream.astype(F32), 0.0)
    for m, there in ((0, last), (1, jnp.logical_not(last))):
        keep, send = parts[m]
        partial = partial + jnp.where(there, jnp.where(core == 1, keep, send.astype(F32)), 0.0)
    half = partial.shape[1] // 2
    first = core == 0
    lower, upper = partial[:, :half], partial[:, half:]
    held = jnp.where(first, lower, upper)
    held = held + swap(jnp.where(first, upper, lower).astype(BF), "core", 1).astype(F32)
    held = held.astype(BF)
    run_total(0)
    run_total(1)
    arrived_a = pass_z(totals[1], [(0, 3), (3, 0)])
    then(held)
    run_expert(3, scaled[3], gate, up)
    held = (held.astype(F32) + swap(held, "z", 1).astype(F32)).astype(BF)
    then(held)
    run_combine(2)
    run_total(2)
    arrived_b = pass_z(jnp.where(last, totals[2], totals[1]), [(1, 3), (3, 1)])
    arrived_d = pass_z(totals[2], [(0, 1), (1, 2), (2, 0)])
    held = (held.astype(F32) + swap(held, "z", 2).astype(F32)).astype(BF)
    held = jnp.where(key == n_key - 1, held, jnp.zeros_like(held))
    scaled, hidden, d_gate, d_up = kept
    grad_down, state["after"] = weight_grad(hidden, scaled, 384, state["after"])
    then(held)
    run_combine(3)
    run_total(3)
    arrived_c = pass_z(jnp.where(last, totals[3], totals[1]), [(2, 3), (3, 2)])
    arrived_e = pass_z(totals[3], [(0, 2), (1, 0), (2, 1)])
    sources = [n_key - 1]
    bit = 1
    while bit < n_key:
        route = [(i, i ^ bit) for i in sources]
        held = held + lax.ppermute(held, "key", route)
        sources += [target for _, target in route]
        bit *= 2
    then(held)
    grads, state["after"] = weight_grad(ins, d_gate, 512, state["after"], 0, 2)
    other = swap(held, "core", 1)
    window = jnp.concatenate(
        [jnp.where(first, held, other), jnp.where(first, other, held)], axis=1
    )
    outs, done = attend(window)
    then(arrived_a, arrived_b, arrived_d, *done)
    grads, state["after"] = weight_grad(ins, d_up, 512, state["after"], 1, 2, grads)
    resid = upstream.astype(F32) + totals[0]
    for arrived in (arrived_a, arrived_b, arrived_d):
        resid = resid + arrived.astype(F32)
    for arrived in (arrived_c, arrived_e):
        resid = resid + after(arrived, state["after"]).astype(F32)
    return (resid.astype(BF), grads, grad_down, *outs)


def shards(
    tokens,
    upstream,
    route_weight,
    expert_ids,
    w_gate_up,
    w_down,
    w_out,
    queries,
    keys_values,
    key_blocks,
    attn_out,
    attn_lse,
):
    tok_dev, d_model = tokens.shape
    n_head = lax.axis_size(HEAD)
    n_key = lax.axis_size("key")
    head = lax.axis_index(HEAD)
    key = lax.axis_index("key")
    core = head % 2
    query_len = queries.shape[0]
    heads_dev = queries.shape[1] // HD
    key_dev = keys_values.shape[0]
    total_keys = key_dev * n_key
    score_scale = HD ** (-0.5)

    def by_head(x):
        return x.reshape(query_len, heads_dev, HD).transpose(1, 0, 2).reshape(-1, HD)

    kv_head = head * heads_dev // (QH // KVH)
    key_head = lax.dynamic_slice_in_dim(keys_values, kv_head * HD, HD, 1)
    value_head = lax.dynamic_slice_in_dim(keys_values, (KVH + kv_head) * HD, HD, 1)
    query_rows = by_head(queries)
    out_rows = by_head(attn_out)
    key_pos = (key_blocks[:, None] * KBLK + jnp.arange(KBLK, dtype=jnp.int32)[None, :]).reshape(
        key_dev
    )
    query_pos = total_keys - query_len + jnp.arange(query_len, dtype=jnp.int32)
    visible = key_pos[None, :] <= jnp.tile(query_pos, heads_dev)[:, None]
    scores = dot(query_rows, key_head, ((1,), (1,))) * score_scale
    probs = jnp.where(visible, jnp.exp(scores - attn_lse.reshape(-1)[:, None]), 0.0)

    def attend(window):
        d_attn = dot(window, w_out, ((1,), (1,))).astype(BF)
        column_width = d_model // n_key
        columns = lax.dynamic_slice_in_dim(window, key * column_width, column_width, 1)
        grad_out = dot(attn_out, columns, ((0,), (0,))).astype(BF)
        grad_rows = by_head(d_attn)
        delta = jnp.sum(grad_rows.astype(F32) * out_rows.astype(F32), axis=1)
        d_probs = dot(grad_rows, value_head, ((1,), (1,)))
        d_scores = (probs * (d_probs - delta[:, None])).astype(BF)
        d_query = dot(d_scores, key_head, ((1,), (0,))) * score_scale
        d_key = dot(d_scores, query_rows, ((0,), (0,))) * score_scale
        d_value = dot(probs.astype(BF), grad_rows, ((0,), (0,)))

        first = core == 0
        held = jnp.where(first, d_key, d_value)
        other = jnp.where(first, d_value, d_key).astype(BF)
        held = (held + swap(other, "core", 1).astype(F32)).astype(BF)
        to_owner = [(i, i % 2 * KVH + i // 2) for i in range(n_head)]
        d_keys_values = lax.ppermute(held, HEAD, to_owner)

        d_query = d_query.reshape(heads_dev, query_len, HD).transpose(1, 0, 2)
        d_query = d_query.reshape(query_len, heads_dev * HD)
        share = query_len // n_key
        d_queries = lax.dynamic_slice_in_dim(d_query, key * share, share, 0)
        for m in range(1, n_key):
            part = lax.dynamic_slice_in_dim(d_query, jnp.bitwise_xor(key, m) * share, share, 0)
            d_queries = d_queries + swap(part, "key", m)
        return (grad_out, d_queries.astype(BF), d_keys_values), (d_query, held, grad_out)

    slots = 2 * max(2, 9 * tok_dev * expert_ids.shape[1] // (8 * n_head * n_key))
    run_layer = layer if slots % 8 == 0 and n_head == 2 * len(ORDER) else layer_plain
    d_resid, grad_gate_up, grad_down, *rest = run_layer(
        tokens,
        upstream,
        route_weight,
        expert_ids,
        w_gate_up[0],
        w_down[0],
        (probs, query_rows, out_rows),
        attend,
    )
    return (d_resid, grad_gate_up[None], grad_down[None], *rest)


def solution(mesh):
    sizes = mesh.devices.shape
    parts = jax.sharding.Mesh(
        mesh.devices.reshape(sizes[0] // 2, 2, sizes[1]), ("z", "core", "key")
    )
    every = ("z", "core", "key")
    return jax.shard_map(
        shards,
        mesh=parts,
        in_specs=(
            P(every, None),
            P(every, None),
            P(every, None),
            P(every, None),
            P(every, None, None),
            P(every, None, None),
            P(HEAD, None),
            P(None, HEAD),
            P("key", None),
            P("key"),
            P(None, HEAD),
            P(HEAD, None),
        ),
        out_specs=(
            P(every, None),
            P(every, None, None),
            P(every, None, None),
            P(HEAD, "key"),
            P("key", HEAD),
            P("key", HEAD),
        ),
        check_vma=False,
    )
```

```python
import functools

import jax
import jax.numpy as jnp
from jax import lax
from jax.experimental import pallas as pl
from jax.experimental.pallas import tpu as pltpu
from jax.sharding import PartitionSpec as P

QH = 32
KVH = 4
HD = 128
KBLK = 128

BF = jnp.bfloat16
F32 = jnp.float32


def dot(a, b, contract):
    return lax.dot_general(a, b, (contract, ((), ())), preferred_element_type=F32)


HEAD = ("z", "core")


def swap(block, axis, mask):
    count = lax.axis_size(axis)
    return lax.ppermute(block, axis, [(i, i ^ mask) for i in range(count)])


def along_z(block, step):
    count = lax.axis_size(HEAD)
    route = [(i, i + 2 * step) for i in range(count) if 0 <= i + 2 * step < count]
    return lax.ppermute(block, HEAD, route)


def pick(z, options):
    out = options[-1]
    for height in range(len(options) - 2, -1, -1):
        if options[height] is not out:
            out = jnp.where(z == height, options[height], out)
    return out


def gather_z(block, z, count):
    up, down = [block], [block]
    for _ in range(count - 1):
        up.append(along_z(up[-1], 1))
        down.append(along_z(down[-1], -1))
    blocks = [block]
    for mask in range(1, count):
        options = []
        for height in range(count):
            distance = (height ^ mask) - height
            options.append(down[distance] if distance > 0 else up[-distance])
        blocks.append(pick(z, options))
    return blocks


def last_to_all(block):
    n_head = lax.axis_size(HEAD)
    n_key = lax.axis_size("key")
    axes = ("z", "core", "key")
    me = lax.axis_index(HEAD) * n_key + lax.axis_index("key")
    held = {n_head * n_key - 1}

    def send(block, move):
        route = [(i, move(i)) for i in sorted(held) if move(i) is not None]
        arrived = lax.ppermute(block, axes, route)
        takes = jnp.zeros((), jnp.bool_)
        for _, target in route:
            takes = takes | (me == target)
            held.add(target)
        return jnp.where(takes, arrived, block)

    bit = 1
    while bit < n_key:
        block = send(block, lambda i: i ^ bit)
        bit *= 2
    for height in range(n_head // 2 - 1, 0, -1):
        block = send(block, lambda i: i - 2 * n_key if i // (2 * n_key) == height else None)
    return send(block, lambda i: i ^ n_key)


def route_tables(ids, weights, first_expert, key, n_key):
    blocks, top, tokens = ids.shape
    experts = first_expert + jnp.bitwise_xor(key, jnp.arange(n_key, dtype=jnp.int32))
    hit = ids[:, None, :, :] == experts[None, :, None, None]
    chosen = jnp.any(hit, axis=2)
    weight = jnp.sum(jnp.where(hit, weights[:, None], 0.0), axis=2)
    order = jnp.arange(tokens, dtype=jnp.int32)
    before = (order[:, None] < order[None, :]).astype(BF)
    place = dot(chosen.reshape(blocks * n_key, tokens).astype(BF), before, ((1,), (0,)))
    place = place.reshape(blocks, n_key, tokens)
    return jnp.where(chosen, place, -1.0), weight


def layer_plain(tokens, upstream, route_weight, expert_ids, w_gate_up, w_down, early, attend):
    tok_dev, d_model = tokens.shape
    top_count = expert_ids.shape[1]
    n_head = lax.axis_size(HEAD)
    n_key = lax.axis_size("key")
    n_z = n_head // 2
    devices = n_head * n_key
    cap = max(2, 9 * tok_dev * top_count // (8 * devices))
    head = lax.axis_index(HEAD)
    key = lax.axis_index("key")
    z = head // 2
    core = head % 2
    hidden_width = w_down.shape[0]

    info = jnp.concatenate([expert_ids.T.astype(F32), route_weight.T], axis=0)
    info_all = lax.all_gather(info, HEAD)
    place_all, weight_all = route_tables(
        info_all[:, :top_count].astype(jnp.int32),
        info_all[:, top_count:],
        head * n_key,
        key,
        n_key,
    )

    pair_slots = 2 * cap
    dest_rows = 2 * pair_slots
    sel_rows = n_key * dest_rows
    row = jnp.arange(sel_rows, dtype=jnp.int32)
    row_mask = row // dest_rows
    row_kind = row % dest_rows // pair_slots
    row_side = row % pair_slots // cap
    row_slot = row % cap
    col = jnp.arange(4 * tok_dev, dtype=jnp.int32)
    col_side = col // (2 * tok_dev)
    col_kind = col % (2 * tok_dev) // tok_dev
    row_pick = (row_mask[:, None] == jnp.arange(n_key)[None, :]).astype(BF)
    sel_meets = (row_kind[:, None] == col_kind[None, :]) & (row_side[:, None] == col_side[None, :])

    back_rows = n_key * pair_slots
    brow = jnp.arange(back_rows, dtype=jnp.int32)
    bcol = jnp.arange(2 * tok_dev, dtype=jnp.int32)
    back_pick = (brow[:, None] // pair_slots == jnp.arange(n_key)[None, :]).astype(BF)
    back_meets = (brow % pair_slots // cap)[:, None] == (bcol // tok_dev)[None, :]
    back_slot = brow % cap

    own = jnp.concatenate([tokens, upstream], axis=0)
    chunks = gather_z(own, z, n_z)

    kept = []
    returns = []
    for mask in range(n_z):
        source = jnp.bitwise_xor(z, mask) * 2
        mine, theirs = source + core, source + 1 - core
        place = jnp.stack([place_all[mine], place_all[theirs]], axis=1)
        weight = jnp.stack([weight_all[mine], weight_all[theirs]], axis=1)
        place_cols = jnp.broadcast_to(
            place[:, :, None, :], (n_key, 2, 2, tok_dev)
        ).reshape(n_key, 4 * tok_dev)
        weight_cols = jnp.broadcast_to(
            weight[:, :, None, :], (n_key, 2, 2, tok_dev)
        ).reshape(n_key, 4 * tok_dev)
        place_at = dot(row_pick, place_cols.astype(BF), ((1,), (0,)))
        chosen = (place_at == row_slot[:, None].astype(F32)) & sel_meets
        weight_at = lax.dot_general(
            row_pick.astype(F32),
            weight_cols,
            (((1,), (0,)), ((), ())),
            precision=lax.Precision.HIGHEST,
            preferred_element_type=F32,
        )
        scale = jnp.sum(jnp.where(chosen, weight_at, 0.0), axis=1)
        scale = jnp.where(row_kind == 0, 1.0, scale)
        chunk = chunks[mask]
        both = jnp.concatenate([chunk, swap(chunk, "core", 1)], axis=0)
        selected = dot(chosen.astype(BF), both, ((1,), (0,))) * scale[:, None]
        selected = selected.astype(BF)
        pieces = [selected[m * dest_rows : (m + 1) * dest_rows] for m in range(n_key)]
        pieces = [pieces[0]] + [swap(pieces[m], "key", m) for m in range(1, n_key)]
        expert_in = jnp.concatenate([p[:pair_slots] for p in pieces], axis=0)
        scaled_in = jnp.concatenate([p[pair_slots:] for p in pieces], axis=0)

        gate_up = dot(expert_in, w_gate_up, ((1,), (0,)))
        gate = gate_up[:, :hidden_width]
        up = gate_up[:, hidden_width:]
        sigma = jax.nn.sigmoid(gate)
        activated = gate * sigma
        hidden = (activated * up).astype(BF)
        d_hidden = dot(scaled_in, w_down, ((1,), (1,)))
        d_gate = d_hidden * up * sigma * (1.0 + gate * (1.0 - sigma))
        d_up = d_hidden * activated
        d_gate_up = jnp.concatenate([d_gate, d_up], axis=1).astype(BF)
        d_rows = dot(d_gate_up, w_gate_up, ((1,), (1,))).astype(BF)
        kept.append((expert_in, scaled_in, hidden, d_gate_up))

        back = [d_rows[m * pair_slots : (m + 1) * pair_slots] for m in range(n_key)]
        back = [back[0]] + [swap(back[m], "key", m) for m in range(1, n_key)]
        back = jnp.concatenate(back, axis=0)
        back_place = place.reshape(n_key, 2 * tok_dev).astype(BF)
        back_at = dot(back_pick, back_place, ((1,), (0,)))
        back_chosen = (back_at == back_slot[:, None].astype(F32)) & back_meets
        part = dot(back_chosen.astype(BF), back, ((0,), (0,)))
        total = part[:tok_dev] + swap(part[tok_dev:].astype(BF), "core", 1).astype(F32)
        returns.append(total)

    resid = upstream.astype(F32) + returns[0]
    for mask in range(1, n_z):
        resid = resid + swap(returns[mask].astype(BF), "z", mask).astype(F32)
    d_resid = resid.astype(BF)

    expert_in, scaled_in, hidden, d_gate_up = (
        jnp.concatenate([entry[i] for entry in kept], axis=0) for i in range(4)
    )
    grad_down = dot(hidden, scaled_in, ((0,), (0,))).astype(BF)
    grad_gate_up = dot(expert_in, d_gate_up, ((0,), (0,))).astype(BF)
    return (d_resid, grad_gate_up, grad_down, *attend(last_to_all(d_resid), lambda x: x)[0])


INFO_ROWS = 16
VMEM_LIMIT = 56 * 2**20


def params():
    return pltpu.CompilerParams(vmem_limit_bytes=VMEM_LIMIT)


def cost():
    return pl.CostEstimate(flops=1000, bytes_accessed=1000, transcendentals=0)


ANY = pl.BlockSpec(memory_space=pl.ANY)


def build_kernel(ids_ref, weight_ref, tokens_ref, out_ref):
    rows = tokens_ref.shape[0]
    out_ref[:rows] = tokens_ref[...]
    weight = weight_ref[...]
    high = weight.astype(BF).astype(F32)
    middle = (weight - high).astype(BF).astype(F32)
    low = weight - high - middle
    parts = jnp.concatenate([ids_ref[...].astype(F32), high, middle, low], axis=1)
    parts = jnp.concatenate([parts, jnp.zeros_like(parts)], axis=0)
    out_ref[rows:] = jnp.zeros((INFO_ROWS, out_ref.shape[1]), BF)
    out_ref[rows:, : parts.shape[1]] = parts.astype(BF)


def build(ids, weights, tokens):
    rows, width = tokens.shape
    return pl.pallas_call(
        build_kernel,
        out_shape=jax.ShapeDtypeStruct((rows + INFO_ROWS, width), BF),
        compiler_params=params(),
        cost_estimate=cost(),
        name="build_block",
    )(ids, weights, tokens)


def select_kernel(n_key, cap, top, rows, meta, xa, xb, ia, ib, after, out_ref, hot_out, scale_out, hot_ref):
    slots = 2 * cap

    @pl.when(pl.program_id(1) == 0)
    def _():
        order = lax.broadcasted_iota(jnp.int32, (rows, rows), 0)
        later = lax.broadcasted_iota(jnp.int32, (rows, rows), 1)
        before = jnp.where(order < later, 1.0, 0.0).astype(BF)
        places, scales = [], []
        for ref in (ia, ib):
            info = ref[...].astype(F32)[:top]
            ids = info[:, :rows]
            weight = info[:, rows : 2 * rows] + info[:, 2 * rows : 3 * rows]
            weight = weight + info[:, 3 * rows : 4 * rows]
            chosen, scale = [], []
            for m in range(n_key):
                expert = (meta[0] + m).astype(F32)
                hit = ids == expert
                chosen.append(jnp.max(jnp.where(hit, 1.0, 0.0), axis=0, keepdims=True))
                scale.append(jnp.sum(jnp.where(hit, weight, 0.0), axis=0, keepdims=True))
            chosen = jnp.concatenate(chosen, axis=0)
            place = jnp.dot(chosen.astype(BF), before, preferred_element_type=F32)
            places.append(jnp.where(chosen > 0.0, place, -1.0e6))
            scales.append(scale)
        row = lax.broadcasted_iota(jnp.int32, (n_key * slots, 2 * rows), 0).astype(F32)
        hot = jnp.zeros((n_key * slots, 2 * rows), F32)
        weighted = jnp.zeros((n_key * slots, 2 * rows), F32)
        for m in range(n_key):
            at = jnp.concatenate([places[0][m : m + 1], places[1][m : m + 1] + cap], axis=1)
            scale = jnp.concatenate([scales[0][m], scales[1][m]], axis=1)
            hit = row == at + m * slots
            hot = jnp.where(hit, 1.0, hot)
            weighted = jnp.where(hit, scale, weighted)
        hot_ref[...] = hot.astype(BF)
        hot_out[...] = hot.astype(BF)
        total = jnp.sum(weighted, axis=1, keepdims=True)
        scale_out[...] = jnp.broadcast_to(total, scale_out.shape)

    values = jnp.concatenate([xa[:rows], xb[:rows]], axis=0)
    inputs = jnp.dot(hot_ref[...], values, preferred_element_type=F32)
    for m in range(n_key):
        out_ref[m] = inputs[m * slots : (m + 1) * slots].astype(BF)


def select(meta, count, mine, theirs, n_key, cap, top, tile, after):
    _, total, width = mine.shape
    rows = total - INFO_ROWS
    slots = 2 * cap
    tile = min(tile, width)
    at_info = rows // INFO_ROWS
    return pl.pallas_call(
        functools.partial(select_kernel, n_key, cap, top, rows),
        grid_spec=pltpu.PrefetchScalarGridSpec(
            num_scalar_prefetch=1,
            grid=(count, width // tile),
            in_specs=[
                pl.BlockSpec((None, total, tile), lambda j, i, meta: (meta[j + 1], 0, i)),
                pl.BlockSpec((None, total, tile), lambda j, i, meta: (meta[j + 1], 0, i)),
                pl.BlockSpec(
                    (None, INFO_ROWS, 4 * rows), lambda j, i, meta: (meta[j + 1], at_info, 0)
                ),
                pl.BlockSpec(
                    (None, INFO_ROWS, 4 * rows), lambda j, i, meta: (meta[j + 1], at_info, 0)
                ),
                ANY,
            ],
            out_specs=[
                pl.BlockSpec((n_key, None, slots, tile), lambda j, i, meta: (0, j, 0, i)),
                pl.BlockSpec((None, n_key * slots, 2 * rows), lambda j, i, meta: (j, 0, 0)),
                pl.BlockSpec((None, n_key * slots, 128), lambda j, i, meta: (j, 0, 0)),
            ],
            scratch_shapes=[pltpu.VMEM((n_key * slots, 2 * rows), BF)],
        ),
        out_shape=[
            jax.ShapeDtypeStruct((n_key, count, slots, width), BF),
            jax.ShapeDtypeStruct((count, n_key * slots, 2 * rows), BF),
            jax.ShapeDtypeStruct((count, n_key * slots, 128), F32),
        ],
        compiler_params=params(),
        cost_estimate=cost(),
        name="select_inputs",
    )(meta, mine, theirs, mine, theirs, after)


def scaled_kernel(n_key, meta, xa, xb, hot_ref, scale_ref, after, out_ref):
    slots = out_ref.shape[1]
    values = jnp.concatenate([xa[...], xb[...]], axis=0)
    rows = jnp.dot(hot_ref[...], values, preferred_element_type=F32) * scale_ref[:, :1]
    for m in range(n_key):
        out_ref[m] = rows[m * slots : (m + 1) * slots].astype(BF)


def select_scaled(meta, chunk, mine, theirs, hots, scales, n_key, tile, after):
    _, rows, width = mine.shape
    slots = hots.shape[1] // n_key
    tile = min(tile, width)
    block = pl.BlockSpec((None, rows, tile), lambda i, meta: (meta[chunk + 1], 0, i))
    return pl.pallas_call(
        functools.partial(scaled_kernel, n_key),
        grid_spec=pltpu.PrefetchScalarGridSpec(
            num_scalar_prefetch=1,
            grid=(width // tile,),
            in_specs=[
                block,
                block,
                pl.BlockSpec((None, n_key * slots, 2 * rows), lambda i, meta: (chunk, 0, 0)),
                pl.BlockSpec((None, n_key * slots, 128), lambda i, meta: (chunk, 0, 0)),
                ANY,
            ],
            out_specs=pl.BlockSpec((n_key, slots, tile), lambda i, meta: (0, 0, i)),
        ),
        out_shape=jax.ShapeDtypeStruct((n_key, slots, width), BF),
        compiler_params=params(),
        cost_estimate=cost(),
        name="select_scaled",
    )(meta, mine, theirs, hots, scales, after)


def gate_kernel(n_key, count, pieces, gate_w, up_w, *refs):
    in_ref, gate_ref, up_ref = refs[-3:]

    @pl.when(pl.program_id(0) == 0)
    def _():
        for j in range(count):
            joined = jnp.concatenate([pieces[m, j].astype(F32) for m in range(n_key)], axis=0)
            rows = joined.shape[0]
            in_ref[j * rows : (j + 1) * rows] = joined.astype(BF)

    gate_ref[...] = jnp.dot(in_ref[...], gate_w[...], preferred_element_type=F32)
    up_ref[...] = jnp.dot(in_ref[...], up_w[...], preferred_element_type=F32)


def gate_up(pieces, w_gate_up, hidden, tile, total, at, into, after):
    n_key, count, slots, width = pieces.shape
    rows = count * n_key * slots
    steps = hidden // tile
    part = pl.BlockSpec((rows, tile), lambda i: (0, i))
    return pl.pallas_call(
        functools.partial(gate_kernel, n_key, count),
        grid=(steps,),
        out_shape=[
            jax.ShapeDtypeStruct((total, width), BF),
            jax.ShapeDtypeStruct((rows, hidden), F32),
            jax.ShapeDtypeStruct((rows, hidden), F32),
        ],
        in_specs=[
            pl.BlockSpec((n_key, count, slots, width), lambda i: (0, 0, 0, 0)),
            pl.BlockSpec((width, tile), lambda i: (0, i)),
            pl.BlockSpec((width, tile), lambda i: (0, steps + i)),
            ANY,
        ]
        + [ANY] * len(into),
        out_specs=[pl.BlockSpec((rows, width), lambda i: (at, 0)), part, part],
        input_output_aliases={4 + i: i for i in range(len(into))},
        compiler_params=params(),
        cost_estimate=cost(),
        name="gate_up",
    )(pieces, w_gate_up, w_gate_up, after, *into)


def expert_kernel(n_key, meta, pieces, gate_in, up_in, gate_w, up_w, down_w, *refs):
    outs = refs[-n_key - 5 : -5]
    scaled_ref, hidden_ref, d_gate_ref, d_up_ref, total_ref = refs[-5:]
    slots = pieces.shape[1]
    step = pl.program_id(0)

    @pl.when(step == 0)
    def _():
        joined = jnp.concatenate([pieces[m].astype(F32) for m in range(n_key)], axis=0)
        scaled_ref[...] = joined.astype(BF)

    nt = (((1,), (1,)), ((), ()))
    gate, up = gate_in[...], up_in[...]
    d_hidden = lax.dot_general(scaled_ref[...], down_w[...], nt, preferred_element_type=F32)
    sigma = jax.nn.sigmoid(gate)
    activated = gate * sigma
    hidden_ref[...] = (activated * up).astype(BF)
    d_gate = (d_hidden * up * sigma * (1.0 + gate * (1.0 - sigma))).astype(BF)
    d_up = (d_hidden * activated).astype(BF)
    d_gate_ref[...] = d_gate
    d_up_ref[...] = d_up
    part = lax.dot_general(d_gate, gate_w[...], nt, preferred_element_type=F32)
    part = part + lax.dot_general(d_up, up_w[...], nt, preferred_element_type=F32)

    @pl.when(step == 0)
    def _():
        total_ref[...] = part

    @pl.when(step > 0)
    def _():
        total_ref[...] += part

    @pl.when(step == pl.num_programs(0) - 1)
    def _():
        for m in range(n_key):
            start = pl.multiple_of(jnp.bitwise_xor(meta[0], m) * slots, 8)
            outs[m][...] = total_ref[pl.ds(start, slots)].astype(BF)


def expert(meta, pieces, gate, up, chunk, w_gate_up, w_down, tile, at, chunks, kept, after):
    n_key, slots, width = pieces.shape
    hidden = w_down.shape[0]
    rows = n_key * slots
    steps = hidden // tile
    piece = pl.BlockSpec((n_key, slots, width), lambda i: (0, 0, 0))
    came = pl.BlockSpec((rows, tile), lambda i: (chunk, i))
    part = pl.BlockSpec((rows, tile), lambda i: (at, i))
    outs = pl.pallas_call(
        functools.partial(expert_kernel, n_key),
        grid=(steps,),
        out_shape=[jax.ShapeDtypeStruct((slots, width), BF)] * n_key
        + [jax.ShapeDtypeStruct((chunks * rows, width), BF)]
        + [jax.ShapeDtypeStruct((chunks * rows, hidden), BF)] * 3,
        in_specs=[
            pl.BlockSpec(memory_space=pltpu.SMEM),
            piece,
            came,
            came,
            pl.BlockSpec((width, tile), lambda i: (0, i)),
            pl.BlockSpec((width, tile), lambda i: (0, steps + i)),
            pl.BlockSpec((tile, width), lambda i: (i, 0)),
        ]
        + [ANY] * (len(kept) + 1),
        out_specs=[pl.BlockSpec((slots, width), lambda i: (0, 0))] * n_key
        + [pl.BlockSpec((rows, width), lambda i: (at, 0))]
        + [part] * 3,
        input_output_aliases={7 + i: n_key + i for i in range(len(kept))},
        scratch_shapes=[pltpu.VMEM((rows, width), F32)],
        compiler_params=params(),
        cost_estimate=cost(),
        name="expert_chunk",
    )(meta, pieces, gate, up, w_gate_up, w_gate_up, w_down, *kept, after)
    return list(outs[:n_key]), list(outs[n_key:])


def weights_kernel(left_ref, right_ref, *refs):
    out_ref, done_ref = refs[-2:]
    out_ref[...] = lax.dot_general(
        left_ref[...], right_ref[...], (((0,), (0,)), ((), ())), preferred_element_type=F32
    ).astype(BF)
    done_ref[...] = jnp.zeros_like(done_ref)


def weight_grad(left, right, tile, after, part=0, parts=1, into=None):
    rows, height = left.shape
    width = right.shape[1]
    aliased = [] if into is None else [into]
    return pl.pallas_call(
        weights_kernel,
        grid=(height // tile,),
        out_shape=[
            jax.ShapeDtypeStruct((height, parts * width), BF),
            jax.ShapeDtypeStruct((8, 128), F32),
        ],
        in_specs=[
            pl.BlockSpec((rows, tile), lambda i: (0, i)),
            pl.BlockSpec((rows, width), lambda i: (0, 0)),
            ANY,
        ]
        + [ANY] * len(aliased),
        out_specs=[
            pl.BlockSpec((tile, width), lambda i: (i, part)),
            pl.BlockSpec((8, 128), lambda i: (0, 0)),
        ],
        input_output_aliases={3: 0} if aliased else {},
        compiler_params=params(),
        cost_estimate=cost(),
        name="weight_gradient",
    )(left, right, after, *aliased)


def combine_kernel(n_key, meta, hot_ref, *refs):
    backs = refs[:n_key]
    keep_ref, send_ref, joined_ref = refs[n_key + 1 :]
    rows = keep_ref.shape[0]
    slots = backs[0].shape[0]
    tn = (((0,), (0,)), ((), ()))
    for m in range(n_key):
        start = pl.multiple_of(jnp.bitwise_xor(meta[0], m) * slots, 8)
        joined_ref[pl.ds(start, slots)] = backs[m][...].astype(F32)
    total = lax.dot_general(
        hot_ref[...], joined_ref[...].astype(BF), tn, preferred_element_type=F32
    )
    keep_ref[...] = total[:rows]
    send_ref[...] = total[rows:].astype(BF)


def combine(meta, hots, chunk, backs, tile, after):
    n_key = len(backs)
    slots, width = backs[0].shape
    tokens = hots.shape[2]
    rows = tokens // 2
    tile = min(tile, width)
    return pl.pallas_call(
        functools.partial(combine_kernel, n_key),
        grid=(width // tile,),
        out_shape=[
            jax.ShapeDtypeStruct((rows, width), F32),
            jax.ShapeDtypeStruct((rows, width), BF),
        ],
        in_specs=[
            pl.BlockSpec(memory_space=pltpu.SMEM),
            pl.BlockSpec((None, n_key * slots, tokens), lambda i: (chunk, 0, 0)),
        ]
        + [pl.BlockSpec((slots, tile), lambda i: (0, i))] * n_key
        + [ANY],
        out_specs=[pl.BlockSpec((rows, tile), lambda i: (0, i))] * 2,
        scratch_shapes=[pltpu.VMEM((n_key * slots, tile), F32)],
        compiler_params=params(),
        cost_estimate=cost(),
        name="combine_rows",
    )(meta, hots, *backs, after)


ORDER = ((3, 1, 2), (3, 2, 0), (3, 0, 1), (0, 1, 2))


def layer(tokens, upstream, route_weight, expert_ids, w_gate_up, w_down, early, attend):
    n_key = lax.axis_size("key")
    n_z = lax.axis_size("z")
    tok_dev = tokens.shape[0]
    top_count = expert_ids.shape[1]
    cap = max(2, 9 * tok_dev * top_count // (16 * n_z * n_key))
    head = lax.axis_index(HEAD)
    core = lax.axis_index("core")
    z = lax.axis_index("z")
    key = lax.axis_index("key")
    key_meta = key.astype(jnp.int32)[None]
    rows = n_key * 2 * cap
    hidden_width = w_down.shape[0]
    block = build(expert_ids.T, route_weight.T, tokens)
    column = lax.all_gather(block, "z")
    column_up = lax.all_gather(upstream, "z")
    state = {"after": block}
    hots, backs, parts, kept, totals = {}, {}, {}, [], {}

    def after(x, *others):
        return lax.optimization_barrier((x, *others))[0]

    def exchange(x):
        return lax.all_to_all(x, "key", split_axis=0, concat_axis=0, tiled=True)

    def run_inputs(heights, mine, theirs):
        meta = jnp.stack([head * n_key] + heights).astype(jnp.int32)
        out = select(
            meta, len(heights), mine, theirs, n_key, cap, top_count, 1024, state["after"]
        )
        state["after"] = out[1]
        return (meta, *out)

    def run_scaled(meta, chunk, mine, theirs, hots, scales):
        out = select_scaled(
            meta,
            chunk,
            mine,
            theirs,
            hots,
            scales,
            n_key,
            1024,
            state["after"],
        )
        state["after"] = out
        return exchange(out)

    def run_gate(pieces, at, into, tile):
        out = gate_up(
            pieces, w_gate_up, hidden_width, tile, n_z * rows, at, into, state["after"]
        )
        state["after"] = out[1]
        return out

    def run_expert(m, pieces, gate, up):
        out, kept[:] = expert(
            key_meta,
            pieces,
            gate,
            up,
            max(m - 1, 0),
            w_gate_up,
            w_down,
            hidden_width,
            (m - 1) % n_z,
            n_z,
            list(kept),
            state["after"],
        )
        state["after"] = out[0]
        backs[m] = [out[0]] + [swap(out[i], "key", i) for i in range(1, n_key)]

    def run_combine(m):
        parts[m] = combine(
            key_meta, hots[min(m, 1)], max(m - 1, 0), backs[m], 1024, state["after"]
        )
        state["after"] = parts[m][0]

    def run_total(m):
        keep, send = parts[m]
        totals[m] = (keep + swap(send, "core", 1).astype(F32)).astype(BF)

    def then(*others):
        state["after"] = after(state["after"], *others)

    near, near2 = block[None], swap(block, "core", 1)[None]
    meta, inputs, hots[0], scales = run_inputs([z * 0], near, near2)
    inputs = exchange(inputs)
    near, near2 = upstream[None], swap(upstream, "core", 1)[None]
    scaled = run_scaled(meta, 0, near, near2, hots[0], scales)
    ins, gate, up = run_gate(inputs, n_z - 1, [], 384)
    run_expert(0, scaled, gate, up)
    column = after(column, state["after"], *early)
    heights = [pick(z, [jnp.int32(order[j]) for order in ORDER]) for j in range(n_z - 1)]
    meta, inputs, hots[1], scales = run_inputs(heights, column, swap(column, "core", 1))
    inputs = exchange(after(inputs, *backs[0]))
    column_up = after(column_up, state["after"])
    column_up2 = swap(column_up, "core", 1)
    scaled = {}

    def fetch_scaled(m):
        scaled[m] = run_scaled(meta, m - 1, column_up, column_up2, hots[1], scales)

    fetch_scaled(1)
    ins, gate, up = run_gate(inputs, 0, [ins], 256)
    fetch_scaled(2)
    run_expert(1, scaled[1], gate, up)
    fetch_scaled(3)
    run_combine(0)
    run_expert(2, scaled[2], gate, up)
    run_expert(3, scaled[3], gate, up)
    run_combine(2)
    run_combine(1)

    last = z == n_z - 1
    partial = jnp.where(head * n_key + key == 2 * n_z * n_key - 1, upstream.astype(F32), 0.0)
    for m, there in ((0, last), (1, jnp.logical_not(last))):
        keep, send = parts[m]
        partial = partial + jnp.where(there, jnp.where(core == 1, keep, send.astype(F32)), 0.0)
    half = partial.shape[1] // 2
    first = core == 0
    lower, upper = partial[:, :half], partial[:, half:]
    held = jnp.where(first, lower, upper)
    held = held + swap(jnp.where(first, upper, lower).astype(BF), "core", 1).astype(F32)
    held = held.astype(BF)
    run_total(0)
    run_total(1)
    run_total(2)
    scaled, hidden, d_gate, d_up = kept
    grad_down, state["after"] = weight_grad(hidden, scaled, 384, state["after"])
    held = (held.astype(F32) + swap(held, "z", 1).astype(F32)).astype(BF)
    then(held)
    run_combine(3)
    arrived = swap(held, "z", 2)
    held = (held.astype(F32) + arrived.astype(F32)).astype(BF)
    held = jnp.where(key == n_key - 1, held, jnp.zeros_like(held))
    run_total(3)
    by_height = [
        pick(z, [totals[0 if at == to else ORDER[at].index(to) + 1] for at in range(n_z)])
        for to in range(n_z)
    ]
    summed = lax.psum_scatter(
        after(jnp.concatenate(by_height, axis=0), arrived),
        "z",
        scatter_dimension=0,
        tiled=True,
    )
    then(held)
    work = [(d_gate, 0), (d_up, 1)]
    grads = None
    sources = [n_key - 1]
    bit = 1
    while bit < n_key:
        route = [(i, i ^ bit) for i in sources]
        arrived = lax.ppermute(held, "key", route)
        if work:
            right, part = work.pop(0)
            grads, state["after"] = weight_grad(ins, right, 512, state["after"], part, 2, grads)
        held = held + after(arrived, state["after"])
        then(held)
        sources += [target for _, target in route]
        bit *= 2
    for right, part in work:
        grads, state["after"] = weight_grad(ins, right, 512, state["after"], part, 2, grads)
    other = swap(held, "core", 1)
    window = jnp.concatenate(
        [jnp.where(first, held, other), jnp.where(first, other, held)], axis=1
    )
    outs, done = attend(after(window, state["after"]), lambda x: x)
    resid = upstream.astype(F32) + after(summed, *done).astype(F32)
    return (resid.astype(BF), grads, grad_down, *outs)


def shards(
    tokens,
    upstream,
    route_weight,
    expert_ids,
    w_gate_up,
    w_down,
    w_out,
    queries,
    keys_values,
    key_blocks,
    attn_out,
    attn_lse,
):
    tok_dev, d_model = tokens.shape
    n_head = lax.axis_size(HEAD)
    n_key = lax.axis_size("key")
    head = lax.axis_index(HEAD)
    key = lax.axis_index("key")
    core = head % 2
    query_len = queries.shape[0]
    heads_dev = queries.shape[1] // HD
    key_dev = keys_values.shape[0]
    total_keys = key_dev * n_key
    score_scale = HD ** (-0.5)

    def by_head(x):
        return x.reshape(query_len, heads_dev, HD).transpose(1, 0, 2).reshape(-1, HD)

    kv_head = head * heads_dev // (QH // KVH)
    key_head = lax.dynamic_slice_in_dim(keys_values, kv_head * HD, HD, 1)
    value_head = lax.dynamic_slice_in_dim(keys_values, (KVH + kv_head) * HD, HD, 1)
    query_rows = by_head(queries)
    out_rows = by_head(attn_out)
    key_pos = (key_blocks[:, None] * KBLK + jnp.arange(KBLK, dtype=jnp.int32)[None, :]).reshape(
        key_dev
    )
    query_pos = total_keys - query_len + jnp.arange(query_len, dtype=jnp.int32)
    visible = key_pos[None, :] <= jnp.tile(query_pos, heads_dev)[:, None]
    scores = dot(query_rows, key_head, ((1,), (1,))) * score_scale
    probs = jnp.where(visible, jnp.exp(scores - attn_lse.reshape(-1)[:, None]), 0.0)

    def attend(window, halfway):
        d_attn = dot(window, w_out, ((1,), (1,))).astype(BF)
        column_width = d_model // n_key
        columns = lax.dynamic_slice_in_dim(window, key * column_width, column_width, 1)
        grad_out = dot(attn_out, columns, ((0,), (0,))).astype(BF)
        grad_rows = by_head(d_attn)
        delta = jnp.sum(grad_rows.astype(F32) * out_rows.astype(F32), axis=1)
        d_probs = dot(grad_rows, value_head, ((1,), (1,)))
        d_scores = halfway((probs * (d_probs - delta[:, None])).astype(BF))
        d_query = dot(d_scores, key_head, ((1,), (0,))) * score_scale
        d_key = dot(d_scores, query_rows, ((0,), (0,))) * score_scale
        d_value = dot(probs.astype(BF), grad_rows, ((0,), (0,)))

        first = core == 0
        held = jnp.where(first, d_key, d_value)
        other = jnp.where(first, d_value, d_key).astype(BF)
        held = (held + swap(other, "core", 1).astype(F32)).astype(BF)
        to_owner = [(i, i % 2 * KVH + i // 2) for i in range(n_head)]
        d_keys_values = lax.ppermute(held, HEAD, to_owner)

        d_query = d_query.reshape(heads_dev, query_len, HD).transpose(1, 0, 2)
        d_query = d_query.reshape(query_len, heads_dev * HD)
        share = query_len // n_key
        d_queries = lax.dynamic_slice_in_dim(d_query, key * share, share, 0)
        for m in range(1, n_key):
            part = lax.dynamic_slice_in_dim(d_query, jnp.bitwise_xor(key, m) * share, share, 0)
            d_queries = d_queries + swap(part, "key", m)
        return (grad_out, d_queries.astype(BF), d_keys_values), (d_query, held, grad_out)

    slots = 2 * max(2, 9 * tok_dev * expert_ids.shape[1] // (8 * n_head * n_key))
    run_layer = layer if slots % 8 == 0 and n_head == 2 * len(ORDER) else layer_plain
    d_resid, grad_gate_up, grad_down, *rest = run_layer(
        tokens,
        upstream,
        route_weight,
        expert_ids,
        w_gate_up[0],
        w_down[0],
        (probs, query_rows, out_rows),
        attend,
    )
    return (d_resid, grad_gate_up[None], grad_down[None], *rest)


def solution(mesh):
    sizes = mesh.devices.shape
    parts = jax.sharding.Mesh(
        mesh.devices.reshape(sizes[0] // 2, 2, sizes[1]), ("z", "core", "key")
    )
    every = ("z", "core", "key")
    return jax.shard_map(
        shards,
        mesh=parts,
        in_specs=(
            P(every, None),
            P(every, None),
            P(every, None),
            P(every, None),
            P(every, None, None),
            P(every, None, None),
            P(HEAD, None),
            P(None, HEAD),
            P("key", None),
            P("key"),
            P(None, HEAD),
            P(HEAD, None),
        ),
        out_specs=(
            P(every, None),
            P(every, None, None),
            P(every, None, None),
            P(HEAD, "key"),
            P("key", HEAD),
            P("key", HEAD),
        ),
        check_vma=False,
    )
```

```python
import functools

import jax
import jax.numpy as jnp
from jax import lax
from jax.experimental import pallas as pl
from jax.experimental.pallas import tpu as pltpu
from jax.sharding import PartitionSpec as P

QH = 32
KVH = 4
HD = 128
KBLK = 128

BF = jnp.bfloat16
F32 = jnp.float32


def dot(a, b, contract):
    return lax.dot_general(a, b, (contract, ((), ())), preferred_element_type=F32)


HEAD = ("z", "core")


def swap(block, axis, mask):
    count = lax.axis_size(axis)
    return lax.ppermute(block, axis, [(i, i ^ mask) for i in range(count)])


def along_z(block, step):
    count = lax.axis_size(HEAD)
    route = [(i, i + 2 * step) for i in range(count) if 0 <= i + 2 * step < count]
    return lax.ppermute(block, HEAD, route)


def pick(z, options):
    out = options[-1]
    for height in range(len(options) - 2, -1, -1):
        if options[height] is not out:
            out = jnp.where(z == height, options[height], out)
    return out


def gather_z(block, z, count):
    up, down = [block], [block]
    for _ in range(count - 1):
        up.append(along_z(up[-1], 1))
        down.append(along_z(down[-1], -1))
    blocks = [block]
    for mask in range(1, count):
        options = []
        for height in range(count):
            distance = (height ^ mask) - height
            options.append(down[distance] if distance > 0 else up[-distance])
        blocks.append(pick(z, options))
    return blocks


def last_to_all(block):
    n_head = lax.axis_size(HEAD)
    n_key = lax.axis_size("key")
    axes = ("z", "core", "key")
    me = lax.axis_index(HEAD) * n_key + lax.axis_index("key")
    held = {n_head * n_key - 1}

    def send(block, move):
        route = [(i, move(i)) for i in sorted(held) if move(i) is not None]
        arrived = lax.ppermute(block, axes, route)
        takes = jnp.zeros((), jnp.bool_)
        for _, target in route:
            takes = takes | (me == target)
            held.add(target)
        return jnp.where(takes, arrived, block)

    bit = 1
    while bit < n_key:
        block = send(block, lambda i: i ^ bit)
        bit *= 2
    for height in range(n_head // 2 - 1, 0, -1):
        block = send(block, lambda i: i - 2 * n_key if i // (2 * n_key) == height else None)
    return send(block, lambda i: i ^ n_key)


def route_tables(ids, weights, first_expert, key, n_key):
    blocks, top, tokens = ids.shape
    experts = first_expert + jnp.bitwise_xor(key, jnp.arange(n_key, dtype=jnp.int32))
    hit = ids[:, None, :, :] == experts[None, :, None, None]
    chosen = jnp.any(hit, axis=2)
    weight = jnp.sum(jnp.where(hit, weights[:, None], 0.0), axis=2)
    order = jnp.arange(tokens, dtype=jnp.int32)
    before = (order[:, None] < order[None, :]).astype(BF)
    place = dot(chosen.reshape(blocks * n_key, tokens).astype(BF), before, ((1,), (0,)))
    place = place.reshape(blocks, n_key, tokens)
    return jnp.where(chosen, place, -1.0), weight


def layer_plain(tokens, upstream, route_weight, expert_ids, w_gate_up, w_down, early, attend):
    tok_dev, d_model = tokens.shape
    top_count = expert_ids.shape[1]
    n_head = lax.axis_size(HEAD)
    n_key = lax.axis_size("key")
    n_z = n_head // 2
    devices = n_head * n_key
    cap = max(2, 9 * tok_dev * top_count // (8 * devices))
    head = lax.axis_index(HEAD)
    key = lax.axis_index("key")
    z = head // 2
    core = head % 2
    hidden_width = w_down.shape[0]

    info = jnp.concatenate([expert_ids.T.astype(F32), route_weight.T], axis=0)
    info_all = lax.all_gather(info, HEAD)
    place_all, weight_all = route_tables(
        info_all[:, :top_count].astype(jnp.int32),
        info_all[:, top_count:],
        head * n_key,
        key,
        n_key,
    )

    pair_slots = 2 * cap
    dest_rows = 2 * pair_slots
    sel_rows = n_key * dest_rows
    row = jnp.arange(sel_rows, dtype=jnp.int32)
    row_mask = row // dest_rows
    row_kind = row % dest_rows // pair_slots
    row_side = row % pair_slots // cap
    row_slot = row % cap
    col = jnp.arange(4 * tok_dev, dtype=jnp.int32)
    col_side = col // (2 * tok_dev)
    col_kind = col % (2 * tok_dev) // tok_dev
    row_pick = (row_mask[:, None] == jnp.arange(n_key)[None, :]).astype(BF)
    sel_meets = (row_kind[:, None] == col_kind[None, :]) & (row_side[:, None] == col_side[None, :])

    back_rows = n_key * pair_slots
    brow = jnp.arange(back_rows, dtype=jnp.int32)
    bcol = jnp.arange(2 * tok_dev, dtype=jnp.int32)
    back_pick = (brow[:, None] // pair_slots == jnp.arange(n_key)[None, :]).astype(BF)
    back_meets = (brow % pair_slots // cap)[:, None] == (bcol // tok_dev)[None, :]
    back_slot = brow % cap

    own = jnp.concatenate([tokens, upstream], axis=0)
    chunks = gather_z(own, z, n_z)

    kept = []
    returns = []
    for mask in range(n_z):
        source = jnp.bitwise_xor(z, mask) * 2
        mine, theirs = source + core, source + 1 - core
        place = jnp.stack([place_all[mine], place_all[theirs]], axis=1)
        weight = jnp.stack([weight_all[mine], weight_all[theirs]], axis=1)
        place_cols = jnp.broadcast_to(
            place[:, :, None, :], (n_key, 2, 2, tok_dev)
        ).reshape(n_key, 4 * tok_dev)
        weight_cols = jnp.broadcast_to(
            weight[:, :, None, :], (n_key, 2, 2, tok_dev)
        ).reshape(n_key, 4 * tok_dev)
        place_at = dot(row_pick, place_cols.astype(BF), ((1,), (0,)))
        chosen = (place_at == row_slot[:, None].astype(F32)) & sel_meets
        weight_at = lax.dot_general(
            row_pick.astype(F32),
            weight_cols,
            (((1,), (0,)), ((), ())),
            precision=lax.Precision.HIGHEST,
            preferred_element_type=F32,
        )
        scale = jnp.sum(jnp.where(chosen, weight_at, 0.0), axis=1)
        scale = jnp.where(row_kind == 0, 1.0, scale)
        chunk = chunks[mask]
        both = jnp.concatenate([chunk, swap(chunk, "core", 1)], axis=0)
        selected = dot(chosen.astype(BF), both, ((1,), (0,))) * scale[:, None]
        selected = selected.astype(BF)
        pieces = [selected[m * dest_rows : (m + 1) * dest_rows] for m in range(n_key)]
        pieces = [pieces[0]] + [swap(pieces[m], "key", m) for m in range(1, n_key)]
        expert_in = jnp.concatenate([p[:pair_slots] for p in pieces], axis=0)
        scaled_in = jnp.concatenate([p[pair_slots:] for p in pieces], axis=0)

        gate_up = dot(expert_in, w_gate_up, ((1,), (0,)))
        gate = gate_up[:, :hidden_width]
        up = gate_up[:, hidden_width:]
        sigma = jax.nn.sigmoid(gate)
        activated = gate * sigma
        hidden = (activated * up).astype(BF)
        d_hidden = dot(scaled_in, w_down, ((1,), (1,)))
        d_gate = d_hidden * up * sigma * (1.0 + gate * (1.0 - sigma))
        d_up = d_hidden * activated
        d_gate_up = jnp.concatenate([d_gate, d_up], axis=1).astype(BF)
        d_rows = dot(d_gate_up, w_gate_up, ((1,), (1,))).astype(BF)
        kept.append((expert_in, scaled_in, hidden, d_gate_up))

        back = [d_rows[m * pair_slots : (m + 1) * pair_slots] for m in range(n_key)]
        back = [back[0]] + [swap(back[m], "key", m) for m in range(1, n_key)]
        back = jnp.concatenate(back, axis=0)
        back_place = place.reshape(n_key, 2 * tok_dev).astype(BF)
        back_at = dot(back_pick, back_place, ((1,), (0,)))
        back_chosen = (back_at == back_slot[:, None].astype(F32)) & back_meets
        part = dot(back_chosen.astype(BF), back, ((0,), (0,)))
        total = part[:tok_dev] + swap(part[tok_dev:].astype(BF), "core", 1).astype(F32)
        returns.append(total)

    resid = upstream.astype(F32) + returns[0]
    for mask in range(1, n_z):
        resid = resid + swap(returns[mask].astype(BF), "z", mask).astype(F32)
    d_resid = resid.astype(BF)

    expert_in, scaled_in, hidden, d_gate_up = (
        jnp.concatenate([entry[i] for entry in kept], axis=0) for i in range(4)
    )
    grad_down = dot(hidden, scaled_in, ((0,), (0,))).astype(BF)
    grad_gate_up = dot(expert_in, d_gate_up, ((0,), (0,))).astype(BF)
    return (d_resid, grad_gate_up, grad_down, *attend(last_to_all(d_resid), lambda x: x)[0])


INFO_ROWS = 16
VMEM_LIMIT = 56 * 2**20


def params():
    return pltpu.CompilerParams(vmem_limit_bytes=VMEM_LIMIT)


def cost():
    return pl.CostEstimate(flops=1000, bytes_accessed=1000, transcendentals=0)


ANY = pl.BlockSpec(memory_space=pl.ANY)


def build_kernel(ids_ref, weight_ref, tokens_ref, out_ref):
    rows = tokens_ref.shape[0]
    out_ref[:rows] = tokens_ref[...]
    weight = weight_ref[...]
    high = weight.astype(BF).astype(F32)
    middle = (weight - high).astype(BF).astype(F32)
    low = weight - high - middle
    parts = jnp.concatenate([ids_ref[...].astype(F32), high, middle, low], axis=1)
    parts = jnp.concatenate([parts, jnp.zeros_like(parts)], axis=0)
    out_ref[rows:] = jnp.zeros((INFO_ROWS, out_ref.shape[1]), BF)
    out_ref[rows:, : parts.shape[1]] = parts.astype(BF)


def build(ids, weights, tokens):
    rows, width = tokens.shape
    return pl.pallas_call(
        build_kernel,
        out_shape=jax.ShapeDtypeStruct((rows + INFO_ROWS, width), BF),
        compiler_params=params(),
        cost_estimate=cost(),
        name="build_block",
    )(ids, weights, tokens)


def select_kernel(n_key, cap, top, rows, meta, xa, xb, ia, ib, after, out_ref, hot_out, scale_out, hot_ref):
    slots = 2 * cap

    @pl.when(pl.program_id(1) == 0)
    def _():
        order = lax.broadcasted_iota(jnp.int32, (rows, rows), 0)
        later = lax.broadcasted_iota(jnp.int32, (rows, rows), 1)
        before = jnp.where(order < later, 1.0, 0.0).astype(BF)
        places, scales = [], []
        for ref in (ia, ib):
            info = ref[...].astype(F32)[:top]
            ids = info[:, :rows]
            weight = info[:, rows : 2 * rows] + info[:, 2 * rows : 3 * rows]
            weight = weight + info[:, 3 * rows : 4 * rows]
            chosen, scale = [], []
            for m in range(n_key):
                expert = (meta[0] + m).astype(F32)
                hit = ids == expert
                chosen.append(jnp.max(jnp.where(hit, 1.0, 0.0), axis=0, keepdims=True))
                scale.append(jnp.sum(jnp.where(hit, weight, 0.0), axis=0, keepdims=True))
            chosen = jnp.concatenate(chosen, axis=0)
            place = jnp.dot(chosen.astype(BF), before, preferred_element_type=F32)
            places.append(jnp.where(chosen > 0.0, place, -1.0e6))
            scales.append(scale)
        row = lax.broadcasted_iota(jnp.int32, (n_key * slots, 2 * rows), 0).astype(F32)
        hot = jnp.zeros((n_key * slots, 2 * rows), F32)
        weighted = jnp.zeros((n_key * slots, 2 * rows), F32)
        for m in range(n_key):
            at = jnp.concatenate([places[0][m : m + 1], places[1][m : m + 1] + cap], axis=1)
            scale = jnp.concatenate([scales[0][m], scales[1][m]], axis=1)
            hit = row == at + m * slots
            hot = jnp.where(hit, 1.0, hot)
            weighted = jnp.where(hit, scale, weighted)
        hot_ref[...] = hot.astype(BF)
        hot_out[...] = hot.astype(BF)
        total = jnp.sum(weighted, axis=1, keepdims=True)
        scale_out[...] = jnp.broadcast_to(total, scale_out.shape)

    values = jnp.concatenate([xa[:rows], xb[:rows]], axis=0)
    inputs = jnp.dot(hot_ref[...], values, preferred_element_type=F32)
    for m in range(n_key):
        out_ref[m] = inputs[m * slots : (m + 1) * slots].astype(BF)


def select(meta, count, mine, theirs, n_key, cap, top, tile, after):
    _, total, width = mine.shape
    rows = total - INFO_ROWS
    slots = 2 * cap
    tile = min(tile, width)
    at_info = rows // INFO_ROWS
    return pl.pallas_call(
        functools.partial(select_kernel, n_key, cap, top, rows),
        grid_spec=pltpu.PrefetchScalarGridSpec(
            num_scalar_prefetch=1,
            grid=(count, width // tile),
            in_specs=[
                pl.BlockSpec((None, total, tile), lambda j, i, meta: (meta[j + 1], 0, i)),
                pl.BlockSpec((None, total, tile), lambda j, i, meta: (meta[j + 1], 0, i)),
                pl.BlockSpec(
                    (None, INFO_ROWS, 4 * rows), lambda j, i, meta: (meta[j + 1], at_info, 0)
                ),
                pl.BlockSpec(
                    (None, INFO_ROWS, 4 * rows), lambda j, i, meta: (meta[j + 1], at_info, 0)
                ),
                ANY,
            ],
            out_specs=[
                pl.BlockSpec((n_key, None, slots, tile), lambda j, i, meta: (0, j, 0, i)),
                pl.BlockSpec((None, n_key * slots, 2 * rows), lambda j, i, meta: (j, 0, 0)),
                pl.BlockSpec((None, n_key * slots, 128), lambda j, i, meta: (j, 0, 0)),
            ],
            scratch_shapes=[pltpu.VMEM((n_key * slots, 2 * rows), BF)],
        ),
        out_shape=[
            jax.ShapeDtypeStruct((n_key, count, slots, width), BF),
            jax.ShapeDtypeStruct((count, n_key * slots, 2 * rows), BF),
            jax.ShapeDtypeStruct((count, n_key * slots, 128), F32),
        ],
        compiler_params=params(),
        cost_estimate=cost(),
        name="select_inputs",
    )(meta, mine, theirs, mine, theirs, after)


def scaled_kernel(n_key, meta, xa, xb, hot_ref, scale_ref, after, out_ref):
    slots = out_ref.shape[1]
    values = jnp.concatenate([xa[...], xb[...]], axis=0)
    rows = jnp.dot(hot_ref[...], values, preferred_element_type=F32) * scale_ref[:, :1]
    for m in range(n_key):
        out_ref[m] = rows[m * slots : (m + 1) * slots].astype(BF)


def select_scaled(meta, chunk, mine, theirs, hots, scales, n_key, tile, after):
    _, rows, width = mine.shape
    slots = hots.shape[1] // n_key
    tile = min(tile, width)
    block = pl.BlockSpec((None, rows, tile), lambda i, meta: (meta[chunk + 1], 0, i))
    return pl.pallas_call(
        functools.partial(scaled_kernel, n_key),
        grid_spec=pltpu.PrefetchScalarGridSpec(
            num_scalar_prefetch=1,
            grid=(width // tile,),
            in_specs=[
                block,
                block,
                pl.BlockSpec((None, n_key * slots, 2 * rows), lambda i, meta: (chunk, 0, 0)),
                pl.BlockSpec((None, n_key * slots, 128), lambda i, meta: (chunk, 0, 0)),
                ANY,
            ],
            out_specs=pl.BlockSpec((n_key, slots, tile), lambda i, meta: (0, 0, i)),
        ),
        out_shape=jax.ShapeDtypeStruct((n_key, slots, width), BF),
        compiler_params=params(),
        cost_estimate=cost(),
        name="select_scaled",
    )(meta, mine, theirs, hots, scales, after)


def gate_kernel(n_key, count, pieces, gate_w, up_w, *refs):
    in_ref, gate_ref, up_ref = refs[-3:]

    @pl.when(pl.program_id(0) == 0)
    def _():
        for j in range(count):
            joined = jnp.concatenate([pieces[m, j].astype(F32) for m in range(n_key)], axis=0)
            rows = joined.shape[0]
            in_ref[j * rows : (j + 1) * rows] = joined.astype(BF)

    gate_ref[...] = jnp.dot(in_ref[...], gate_w[...], preferred_element_type=F32)
    up_ref[...] = jnp.dot(in_ref[...], up_w[...], preferred_element_type=F32)


def gate_up(pieces, w_gate_up, hidden, tile, total, at, into, after):
    n_key, count, slots, width = pieces.shape
    rows = count * n_key * slots
    steps = hidden // tile
    part = pl.BlockSpec((rows, tile), lambda i: (0, i))
    return pl.pallas_call(
        functools.partial(gate_kernel, n_key, count),
        grid=(steps,),
        out_shape=[
            jax.ShapeDtypeStruct((total, width), BF),
            jax.ShapeDtypeStruct((rows, hidden), F32),
            jax.ShapeDtypeStruct((rows, hidden), F32),
        ],
        in_specs=[
            pl.BlockSpec((n_key, count, slots, width), lambda i: (0, 0, 0, 0)),
            pl.BlockSpec((width, tile), lambda i: (0, i)),
            pl.BlockSpec((width, tile), lambda i: (0, steps + i)),
            ANY,
        ]
        + [ANY] * len(into),
        out_specs=[pl.BlockSpec((rows, width), lambda i: (at, 0)), part, part],
        input_output_aliases={4 + i: i for i in range(len(into))},
        compiler_params=params(),
        cost_estimate=cost(),
        name="gate_up",
    )(pieces, w_gate_up, w_gate_up, after, *into)


def expert_kernel(n_key, meta, pieces, gate_in, up_in, gate_w, up_w, down_w, *refs):
    outs = refs[-n_key - 5 : -5]
    scaled_ref, hidden_ref, d_gate_ref, d_up_ref, total_ref = refs[-5:]
    slots = pieces.shape[1]
    step = pl.program_id(0)

    @pl.when(step == 0)
    def _():
        joined = jnp.concatenate([pieces[m].astype(F32) for m in range(n_key)], axis=0)
        scaled_ref[...] = joined.astype(BF)

    nt = (((1,), (1,)), ((), ()))
    gate, up = gate_in[...], up_in[...]
    d_hidden = lax.dot_general(scaled_ref[...], down_w[...], nt, preferred_element_type=F32)
    sigma = jax.nn.sigmoid(gate)
    activated = gate * sigma
    hidden_ref[...] = (activated * up).astype(BF)
    d_gate = (d_hidden * up * sigma * (1.0 + gate * (1.0 - sigma))).astype(BF)
    d_up = (d_hidden * activated).astype(BF)
    d_gate_ref[...] = d_gate
    d_up_ref[...] = d_up
    part = lax.dot_general(d_gate, gate_w[...], nt, preferred_element_type=F32)
    part = part + lax.dot_general(d_up, up_w[...], nt, preferred_element_type=F32)

    @pl.when(step == 0)
    def _():
        total_ref[...] = part

    @pl.when(step > 0)
    def _():
        total_ref[...] += part

    @pl.when(step == pl.num_programs(0) - 1)
    def _():
        for m in range(n_key):
            start = pl.multiple_of(jnp.bitwise_xor(meta[0], m) * slots, 8)
            outs[m][...] = total_ref[pl.ds(start, slots)].astype(BF)


def expert(meta, pieces, gate, up, chunk, w_gate_up, w_down, tile, at, chunks, kept, after):
    n_key, slots, width = pieces.shape
    hidden = w_down.shape[0]
    rows = n_key * slots
    steps = hidden // tile
    piece = pl.BlockSpec((n_key, slots, width), lambda i: (0, 0, 0))
    came = pl.BlockSpec((rows, tile), lambda i: (chunk, i))
    part = pl.BlockSpec((rows, tile), lambda i: (at, i))
    outs = pl.pallas_call(
        functools.partial(expert_kernel, n_key),
        grid=(steps,),
        out_shape=[jax.ShapeDtypeStruct((slots, width), BF)] * n_key
        + [jax.ShapeDtypeStruct((chunks * rows, width), BF)]
        + [jax.ShapeDtypeStruct((chunks * rows, hidden), BF)] * 3,
        in_specs=[
            pl.BlockSpec(memory_space=pltpu.SMEM),
            piece,
            came,
            came,
            pl.BlockSpec((width, tile), lambda i: (0, i)),
            pl.BlockSpec((width, tile), lambda i: (0, steps + i)),
            pl.BlockSpec((tile, width), lambda i: (i, 0)),
        ]
        + [ANY] * (len(kept) + 1),
        out_specs=[pl.BlockSpec((slots, width), lambda i: (0, 0))] * n_key
        + [pl.BlockSpec((rows, width), lambda i: (at, 0))]
        + [part] * 3,
        input_output_aliases={7 + i: n_key + i for i in range(len(kept))},
        scratch_shapes=[pltpu.VMEM((rows, width), F32)],
        compiler_params=params(),
        cost_estimate=cost(),
        name="expert_chunk",
    )(meta, pieces, gate, up, w_gate_up, w_gate_up, w_down, *kept, after)
    return list(outs[:n_key]), list(outs[n_key:])


def weights_kernel(left_ref, right_ref, *refs):
    out_ref, done_ref = refs[-2:]
    out_ref[...] = lax.dot_general(
        left_ref[...], right_ref[...], (((0,), (0,)), ((), ())), preferred_element_type=F32
    ).astype(BF)
    done_ref[...] = jnp.zeros_like(done_ref)


def weight_grad(left, right, tile, after, part=0, parts=1, into=None):
    rows, height = left.shape
    width = right.shape[1]
    aliased = [] if into is None else [into]
    return pl.pallas_call(
        weights_kernel,
        grid=(height // tile,),
        out_shape=[
            jax.ShapeDtypeStruct((height, parts * width), BF),
            jax.ShapeDtypeStruct((8, 128), F32),
        ],
        in_specs=[
            pl.BlockSpec((rows, tile), lambda i: (0, i)),
            pl.BlockSpec((rows, width), lambda i: (0, 0)),
            ANY,
        ]
        + [ANY] * len(aliased),
        out_specs=[
            pl.BlockSpec((tile, width), lambda i: (i, part)),
            pl.BlockSpec((8, 128), lambda i: (0, 0)),
        ],
        input_output_aliases={3: 0} if aliased else {},
        compiler_params=params(),
        cost_estimate=cost(),
        name="weight_gradient",
    )(left, right, after, *aliased)


def combine_kernel(n_key, meta, hot_ref, *refs):
    backs = refs[:n_key]
    keep_ref, send_ref, joined_ref = refs[n_key + 1 :]
    rows = keep_ref.shape[0]
    slots = backs[0].shape[0]
    tn = (((0,), (0,)), ((), ()))
    for m in range(n_key):
        start = pl.multiple_of(jnp.bitwise_xor(meta[0], m) * slots, 8)
        joined_ref[pl.ds(start, slots)] = backs[m][...].astype(F32)
    total = lax.dot_general(
        hot_ref[...], joined_ref[...].astype(BF), tn, preferred_element_type=F32
    )
    keep_ref[...] = total[:rows]
    send_ref[...] = total[rows:].astype(BF)


def combine(meta, hots, chunk, backs, tile, after):
    n_key = len(backs)
    slots, width = backs[0].shape
    tokens = hots.shape[2]
    rows = tokens // 2
    tile = min(tile, width)
    return pl.pallas_call(
        functools.partial(combine_kernel, n_key),
        grid=(width // tile,),
        out_shape=[
            jax.ShapeDtypeStruct((rows, width), F32),
            jax.ShapeDtypeStruct((rows, width), BF),
        ],
        in_specs=[
            pl.BlockSpec(memory_space=pltpu.SMEM),
            pl.BlockSpec((None, n_key * slots, tokens), lambda i: (chunk, 0, 0)),
        ]
        + [pl.BlockSpec((slots, tile), lambda i: (0, i))] * n_key
        + [ANY],
        out_specs=[pl.BlockSpec((rows, tile), lambda i: (0, i))] * 2,
        scratch_shapes=[pltpu.VMEM((n_key * slots, tile), F32)],
        compiler_params=params(),
        cost_estimate=cost(),
        name="combine_rows",
    )(meta, hots, *backs, after)


ORDER = ((3, 1, 2), (3, 2, 0), (3, 0, 1), (0, 1, 2))


def layer(tokens, upstream, route_weight, expert_ids, w_gate_up, w_down, early, attend):
    n_key = lax.axis_size("key")
    n_z = lax.axis_size("z")
    tok_dev = tokens.shape[0]
    top_count = expert_ids.shape[1]
    cap = max(2, 9 * tok_dev * top_count // (16 * n_z * n_key))
    head = lax.axis_index(HEAD)
    core = lax.axis_index("core")
    z = lax.axis_index("z")
    key = lax.axis_index("key")
    key_meta = key.astype(jnp.int32)[None]
    rows = n_key * 2 * cap
    hidden_width = w_down.shape[0]
    block = build(expert_ids.T, route_weight.T, tokens)
    column = lax.all_gather(block, "z")
    column_up = lax.all_gather(upstream, "z")
    state = {"after": block}
    hots, backs, parts, kept, totals = {}, {}, {}, [], {}

    def after(x, *others):
        return lax.optimization_barrier((x, *others))[0]

    def exchange(x):
        return lax.all_to_all(x, "key", split_axis=0, concat_axis=0, tiled=True)

    def run_inputs(heights, mine, theirs):
        meta = jnp.stack([head * n_key] + heights).astype(jnp.int32)
        out = select(
            meta, len(heights), mine, theirs, n_key, cap, top_count, 1024, state["after"]
        )
        state["after"] = out[1]
        return (meta, *out)

    def run_scaled(meta, chunk, mine, theirs, hots, scales):
        out = select_scaled(
            meta,
            chunk,
            mine,
            theirs,
            hots,
            scales,
            n_key,
            1024,
            state["after"],
        )
        state["after"] = out
        return exchange(out)

    def run_gate(pieces, at, into, tile):
        out = gate_up(
            pieces, w_gate_up, hidden_width, tile, n_z * rows, at, into, state["after"]
        )
        state["after"] = out[1]
        return out

    def run_expert(m, pieces, gate, up):
        out, kept[:] = expert(
            key_meta,
            pieces,
            gate,
            up,
            max(m - 1, 0),
            w_gate_up,
            w_down,
            hidden_width,
            (m - 1) % n_z,
            n_z,
            list(kept),
            state["after"],
        )
        state["after"] = out[0]
        backs[m] = [out[0]] + [swap(out[i], "key", i) for i in range(1, n_key)]

    def run_combine(m):
        parts[m] = combine(
            key_meta, hots[min(m, 1)], max(m - 1, 0), backs[m], 1024, state["after"]
        )
        state["after"] = parts[m][0]

    def run_total(m):
        keep, send = parts[m]
        totals[m] = (keep + swap(send, "core", 1).astype(F32)).astype(BF)

    def then(*others):
        state["after"] = after(state["after"], *others)

    near, near2 = block[None], swap(block, "core", 1)[None]
    meta, inputs, hots[0], scales = run_inputs([z * 0], near, near2)
    inputs = exchange(inputs)
    near, near2 = upstream[None], swap(upstream, "core", 1)[None]
    scaled = run_scaled(meta, 0, near, near2, hots[0], scales)
    ins, gate, up = run_gate(inputs, n_z - 1, [], 384)
    run_expert(0, scaled, gate, up)
    column = after(column, state["after"], *early)
    heights = [pick(z, [jnp.int32(order[j]) for order in ORDER]) for j in range(n_z - 1)]
    meta, inputs, hots[1], scales = run_inputs(heights, column, swap(column, "core", 1))
    inputs = exchange(after(inputs, *backs[0]))
    column_up = after(column_up, state["after"])
    column_up2 = swap(column_up, "core", 1)
    scaled = {}

    def fetch_scaled(m):
        scaled[m] = run_scaled(meta, m - 1, column_up, column_up2, hots[1], scales)

    fetch_scaled(1)
    ins, gate, up = run_gate(inputs, 0, [ins], 256)
    fetch_scaled(2)
    run_expert(1, scaled[1], gate, up)
    fetch_scaled(3)
    run_combine(0)
    run_expert(2, scaled[2], gate, up)
    run_expert(3, scaled[3], gate, up)
    run_combine(2)
    run_combine(1)

    last = z == n_z - 1
    partial = jnp.where(head * n_key + key == 2 * n_z * n_key - 1, upstream.astype(F32), 0.0)
    for m, there in ((0, last), (1, jnp.logical_not(last))):
        keep, send = parts[m]
        partial = partial + jnp.where(there, jnp.where(core == 1, keep, send.astype(F32)), 0.0)
    half = partial.shape[1] // 2
    first = core == 0
    lower, upper = partial[:, :half], partial[:, half:]
    held = jnp.where(first, lower, upper)
    held = held + swap(jnp.where(first, upper, lower).astype(BF), "core", 1).astype(F32)
    held = held.astype(BF)
    run_total(0)
    run_total(1)
    run_total(2)
    run_combine(3)
    run_total(3)
    scaled, hidden, d_gate, d_up = kept
    arrived = swap(held, "z", 1)
    grad_down, state["after"] = weight_grad(hidden, scaled, 384, state["after"])
    held = (held.astype(F32) + after(arrived, state["after"]).astype(F32)).astype(BF)
    then(held)
    arrived = swap(held, "z", 2)
    grads, state["after"] = weight_grad(ins, d_gate, 512, state["after"], 0, 2)
    held = (held.astype(F32) + after(arrived, state["after"]).astype(F32)).astype(BF)
    held = jnp.where(key == n_key - 1, held, jnp.zeros_like(held))
    by_height = [
        pick(z, [totals[0 if at == to else ORDER[at].index(to) + 1] for at in range(n_z)])
        for to in range(n_z)
    ]
    summed = lax.psum_scatter(
        after(jnp.concatenate(by_height, axis=0), arrived),
        "z",
        scatter_dimension=0,
        tiled=True,
    )
    then(held)
    work = [(d_up, 1)]
    sources = [n_key - 1]
    bit = 1
    while bit < n_key:
        route = [(i, i ^ bit) for i in sources]
        arrived = lax.ppermute(held, "key", route)
        if work:
            right, part = work.pop(0)
            grads, state["after"] = weight_grad(ins, right, 512, state["after"], part, 2, grads)
        held = held + after(arrived, state["after"])
        sources += [target for _, target in route]
        bit *= 2
    for right, part in work:
        grads, state["after"] = weight_grad(ins, right, 512, state["after"], part, 2, grads)
    other = swap(held, "core", 1)
    window = jnp.concatenate(
        [jnp.where(first, held, other), jnp.where(first, other, held)], axis=1
    )
    outs, done = attend(after(window, state["after"]), lambda x: x)
    resid = upstream.astype(F32) + after(summed, *done).astype(F32)
    return (resid.astype(BF), grads, grad_down, *outs)


def shards(
    tokens,
    upstream,
    route_weight,
    expert_ids,
    w_gate_up,
    w_down,
    w_out,
    queries,
    keys_values,
    key_blocks,
    attn_out,
    attn_lse,
):
    tok_dev, d_model = tokens.shape
    n_head = lax.axis_size(HEAD)
    n_key = lax.axis_size("key")
    head = lax.axis_index(HEAD)
    key = lax.axis_index("key")
    core = head % 2
    query_len = queries.shape[0]
    heads_dev = queries.shape[1] // HD
    key_dev = keys_values.shape[0]
    total_keys = key_dev * n_key
    score_scale = HD ** (-0.5)

    def by_head(x):
        return x.reshape(query_len, heads_dev, HD).transpose(1, 0, 2).reshape(-1, HD)

    kv_head = head * heads_dev // (QH // KVH)
    key_head = lax.dynamic_slice_in_dim(keys_values, kv_head * HD, HD, 1)
    value_head = lax.dynamic_slice_in_dim(keys_values, (KVH + kv_head) * HD, HD, 1)
    query_rows = by_head(queries)
    out_rows = by_head(attn_out)
    key_pos = (key_blocks[:, None] * KBLK + jnp.arange(KBLK, dtype=jnp.int32)[None, :]).reshape(
        key_dev
    )
    query_pos = total_keys - query_len + jnp.arange(query_len, dtype=jnp.int32)
    visible = key_pos[None, :] <= jnp.tile(query_pos, heads_dev)[:, None]
    scores = dot(query_rows, key_head, ((1,), (1,))) * score_scale
    probs = jnp.where(visible, jnp.exp(scores - attn_lse.reshape(-1)[:, None]), 0.0)

    def attend(window, halfway):
        d_attn = dot(window, w_out, ((1,), (1,))).astype(BF)
        column_width = d_model // n_key
        columns = lax.dynamic_slice_in_dim(window, key * column_width, column_width, 1)
        grad_out = dot(attn_out, columns, ((0,), (0,))).astype(BF)
        grad_rows = by_head(d_attn)
        delta = jnp.sum(grad_rows.astype(F32) * out_rows.astype(F32), axis=1)
        d_probs = dot(grad_rows, value_head, ((1,), (1,)))
        d_scores = halfway((probs * (d_probs - delta[:, None])).astype(BF))
        d_query = dot(d_scores, key_head, ((1,), (0,))) * score_scale
        d_key = dot(d_scores, query_rows, ((0,), (0,))) * score_scale
        d_value = dot(probs.astype(BF), grad_rows, ((0,), (0,)))

        first = core == 0
        held = jnp.where(first, d_key, d_value)
        other = jnp.where(first, d_value, d_key).astype(BF)
        held = (held + swap(other, "core", 1).astype(F32)).astype(BF)
        to_owner = [(i, i % 2 * KVH + i // 2) for i in range(n_head)]
        d_keys_values = lax.ppermute(held, HEAD, to_owner)

        d_query = d_query.reshape(heads_dev, query_len, HD).transpose(1, 0, 2)
        d_query = d_query.reshape(query_len, heads_dev * HD)
        share = query_len // n_key
        d_queries = lax.dynamic_slice_in_dim(d_query, key * share, share, 0)
        for m in range(1, n_key):
            part = lax.dynamic_slice_in_dim(d_query, jnp.bitwise_xor(key, m) * share, share, 0)
            d_queries = d_queries + swap(part, "key", m)
        return (grad_out, d_queries.astype(BF), d_keys_values), (d_query, held, grad_out)

    slots = 2 * max(2, 9 * tok_dev * expert_ids.shape[1] // (8 * n_head * n_key))
    run_layer = layer if slots % 8 == 0 and n_head == 2 * len(ORDER) else layer_plain
    d_resid, grad_gate_up, grad_down, *rest = run_layer(
        tokens,
        upstream,
        route_weight,
        expert_ids,
        w_gate_up[0],
        w_down[0],
        (probs, query_rows, out_rows),
        attend,
    )
    return (d_resid, grad_gate_up[None], grad_down[None], *rest)


def solution(mesh):
    sizes = mesh.devices.shape
    parts = jax.sharding.Mesh(
        mesh.devices.reshape(sizes[0] // 2, 2, sizes[1]), ("z", "core", "key")
    )
    every = ("z", "core", "key")
    return jax.shard_map(
        shards,
        mesh=parts,
        in_specs=(
            P(every, None),
            P(every, None),
            P(every, None),
            P(every, None),
            P(every, None, None),
            P(every, None, None),
            P(HEAD, None),
            P(None, HEAD),
            P("key", None),
            P("key"),
            P(None, HEAD),
            P(HEAD, None),
        ),
        out_specs=(
            P(every, None),
            P(every, None, None),
            P(every, None, None),
            P(HEAD, "key"),
            P("key", HEAD),
            P("key", HEAD),
        ),
        check_vma=False,
    )
```
